512 devices in a mesh: section: 32 (over y, z_hi), tensor: 16 (over x, z_lo, core).
Axes of the slice: x: 4, y: 8, z: 8 (z_hi: 4, z_lo: 2; z = z_hi * 2 + z_lo), core: 2. Of those that a mesh axis runs over, the one named last changes fastest.
Arguments:
- queries: bfloat16 [16384, 8192], P('section', 'tensor'), may hold values from -160 to 160
- keys: bfloat16 [4096, 1024], P('section'), may hold values from -8 to 8
- values: bfloat16 [4096, 1024], P('section'), may hold values from -6 to 6
- d_out: bfloat16 [16384, 8192], P('section', 'tensor'), may hold values from -6 to 6
- gate: float32 [1], replicated, may hold values from 0.3 to 1.5
- tiles: int32 [8], replicated, may hold values from 1 to 4, as said below
- text_len: int32 [8], replicated, may hold values from 512 to 2048, as said below
Outputs:
- d_queries: bfloat16 [16384, 8192], P('section', 'tensor')
- d_keys: float32 [4096, 1024], P(('section', 'tensor'))
- d_values: float32 [4096, 1024], P(('section', 'tensor'))
The draws below stay inside these ranges and needn't reach their ends.
Inputs may be any that keep to these rules, and one draw needn't show every extreme that they name: Sample 0 has 4 tiles and at least one other sample has 1. `text_len`: at least one sample fills all 2048 text positions.
All inputs are finite; a program needn't handle non-finite values.
Results may differ from the reference program's by a relative error of at most 0.013.
Values may be sent and summed in bfloat16 or wider, within the bound.
No kernel may reach another device: no remote copies, remote signals or barrier semaphores. Data moves between devices by JAX's collectives and lax.ppermute only.
A program may use at most 64 MiB of HBM per device.

```python
import jax
import jax.numpy as jnp
from jax import lax

HEADS = 64
KVH = 8
HD = 128
SAMPLES = 8
TILE = 128
TILES_MAX = 4
TXT = 2048
IMG = 512


def shared_keys(key):
    base = jax.random.normal(key, (SAMPLES * IMG, KVH * HD), jnp.float32)
    return jnp.clip(base, -8.0, 8.0)


def draw_keys(key, part):
    base = shared_keys(key)
    return base.astype(jnp.bfloat16)


def draw_queries(key, part):
    key = jax.random.fold_in(key, 2)
    drawn = jax.random.normal(key, (SAMPLES * TXT, HEADS * HD), jnp.float32)
    drawn = jnp.clip(drawn, -8.0, 8.0)
    return drawn.astype(jnp.bfloat16)


def draw_tiles(key, part):
    key = jax.random.fold_in(key, 3)
    counts = jax.random.randint(key, (SAMPLES,), 1, TILES_MAX + 1)
    single = jax.random.randint(jax.random.fold_in(key, 1), (), 1, SAMPLES)
    index = jnp.arange(SAMPLES, dtype=jnp.int32)
    counts = jnp.where(index == 0, TILES_MAX, counts)
    counts = jnp.where(index == single, 1, counts)
    return counts.astype(jnp.int32)


def draw_text_len(key, part):
    key = jax.random.fold_in(key, 4)
    lengths = jax.random.randint(key, (SAMPLES,), TXT // 4, TXT + 1)
    which = jax.random.randint(jax.random.fold_in(key, 1), (), 0, SAMPLES)
    index = jnp.arange(SAMPLES, dtype=jnp.int32)
    return jnp.where(index == which, TXT, lengths).astype(jnp.int32)


def block_scale(rng, shape, shards, low, top_value):
    loudness, own = 1.0, jax.random.fold_in(rng, 6)
    for axis_at, shards_of in shards:
        draws = jnp.exp(jax.random.uniform(jax.random.fold_in(own, axis_at), (shards_of,), jnp.float32, low / len(shards), top_value / len(shards)))
        loudness = loudness * jnp.repeat(draws, shape[axis_at] // shards_of).reshape([-1 if axis == axis_at else 1 for axis in range(len(shape))])
    return loudness


def noise(own_key, dims, spread, bound, split=(), kind=jnp.bfloat16):
    loudness = block_scale(own_key, dims, split, -0.22, 0.18) if split else 1.0
    entries = jax.random.normal(own_key, dims, jnp.float32) * spread * loudness
    return jnp.minimum(jnp.maximum(entries, -bound), bound).astype(kind)


def setup_inputs(seed: int = 0) -> dict:
    splits = jax.random.split(jax.random.key(seed), 8)
    queries = draw_queries(jax.random.fold_in(splits[7], 71), 0)
    keys = draw_keys(jax.random.fold_in(splits[7], 71), 0)
    values = noise(splits[2], (SAMPLES * IMG, KVH * HD), 1.0, 6.0, ((0, 32),))
    d_out = noise(splits[3], (SAMPLES * TXT, HEADS * HD), 1.0, 6.0, ((0, 32), (1, 16)))
    gate = jnp.clip(jax.random.uniform(splits[4], (1,), jnp.float32, 0.3, 1.5), 0.3, 1.5)
    tiles = draw_tiles(jax.random.fold_in(splits[7], 71), 0)
    text_len = draw_text_len(jax.random.fold_in(splits[7], 71), 0)
    return dict(queries=queries, keys=keys, values=values, d_out=d_out, gate=gate, tiles=tiles, text_len=text_len)


def reference(queries, keys, values, d_out, gate, tiles, text_len):
    share = HEADS // KVH
    scale = HD ** -0.5
    factor = jnp.tanh(gate[0])
    q_all = queries.reshape(SAMPLES, TXT, KVH, share, HD)
    k_all = keys.reshape(SAMPLES, IMG, KVH, HD)
    v_all = values.reshape(SAMPLES, IMG, KVH, HD)
    o_all = d_out.reshape(SAMPLES, TXT, KVH, share, HD)

    def one_sample(items):
        q_blk, k_blk, v_blk, o_blk, n_tiles, n_text = items
        live_rows = jnp.arange(TXT, dtype=jnp.int32) < n_text
        live_cols = jnp.arange(IMG, dtype=jnp.int32) < n_tiles * TILE
        scaled = jnp.where(live_rows[:, None, None, None], factor * o_blk.astype(jnp.float32), 0.0).astype(jnp.bfloat16)
        qf = q_blk.astype(jnp.float32)
        kf = k_blk.astype(jnp.float32)
        vf = v_blk.astype(jnp.float32)
        sf = scaled.astype(jnp.float32)
        score = jnp.einsum('tkgd,jkd->kgtj', qf, kf) * scale
        score = jnp.where(live_cols, score, -1e30)
        top = jnp.max(score, axis=-1, keepdims=True)
        expo = jnp.exp(score - top)
        prob = expo / jnp.sum(expo, axis=-1, keepdims=True)
        prob_b = prob.astype(jnp.bfloat16)
        pf = prob_b.astype(jnp.float32)
        attn = jnp.einsum('kgtj,jkd->tkgd', pf, vf)
        delta = jnp.transpose(jnp.sum(sf * attn, axis=-1), (1, 2, 0))
        dprob = jnp.einsum('tkgd,jkd->kgtj', sf, vf)
        dscore = (prob * (dprob - delta[..., None]) * scale).astype(jnp.bfloat16)
        df = dscore.astype(jnp.float32)
        dq = jnp.einsum('kgtj,jkd->tkgd', df, kf).astype(jnp.bfloat16)
        dk = jnp.einsum('kgtj,tkgd->jkd', df, qf)
        dv = jnp.einsum('kgtj,tkgd->jkd', pf, sf)
        return dq, dk, dv

    dq, dk, dv = lax.map(one_sample, (q_all, k_all, v_all, o_all, tiles, text_len))
    return (dq.reshape(SAMPLES * TXT, HEADS * HD), dk.reshape(SAMPLES * IMG, KVH * HD), dv.reshape(SAMPLES * IMG, KVH * HD))
```

```python
import jax
import jax.numpy as jnp
from jax import lax
from jax.experimental import pallas as pl
from jax.experimental.pallas import tpu as pltpu
from jax.sharding import Mesh, PartitionSpec as P

HD = 128
TILE = 128
SCALE = HD**-0.5
LOG2E = 1.4426950408889634
AXES = ("y", "zh", "x", "zl", "c")
SIZES = (8, 4, 4, 2, 2)
BLOCKS = 4
HEADS_X = 2
PLANE = 64
GROUPS = ((1, 2, 4, 7), (0, 3, 5, 6))
NT = (((1,), (1,)), ((), ()))
VMEM = pl.BlockSpec(memory_space=pltpu.VMEM)
SMEM = pl.BlockSpec(memory_space=pltpu.SMEM)
ANY = pl.BlockSpec(memory_space=pl.ANY)


def pick_kernel(keys, values, out, sems):
    x, zh, zl = lax.axis_index("x"), lax.axis_index("zh"), lax.axis_index("zl")
    first = [z % 2 for z in GROUPS[0]]
    mine = jnp.where((zh == 0) | (zh == 3), 1, 0)
    group = jnp.where(mine == zl, 0, 1)
    copies = []
    for j in range(BLOCKS):
        lo = jnp.where(group == 0, first[j], 1 - first[j])
        column = pl.ds(pl.multiple_of((x * HEADS_X + lo) * HD, HD), HD)
        for k, source in enumerate((keys, values)):
            copies.append(
                pltpu.make_async_copy(source.at[:, column], out.at[j, k], sems.at[j, k])
            )
    for copy in copies:
        copy.start()
    for copy in copies:
        copy.wait()


def main_kernel(tiles, text_len, gate, kv, queries, d_out, d_queries, partial, keys_t, acc_k, acc_v):
    f32, bf16 = jnp.float32, jnp.bfloat16
    y, zh = lax.axis_index("y"), lax.axis_index("zh")
    n_tiles, n_text = tiles[y], text_len[y]
    rows, heads = queries.shape[0], queries.shape[1] // HD
    factor = jnp.tanh(jnp.full((8, HD), gate[0], f32))[0:1, 0:1]
    keys = jnp.concatenate([kv[b, 0] for b in range(BLOCKS)], 0)
    values = jnp.concatenate([kv[b, 1] for b in range(BLOCKS)], 0)
    keys_t[...] = keys.T
    live = lax.broadcasted_iota(jnp.int32, (rows, HD), 0) + zh * rows < n_text
    for h in range(heads):
        cols = pl.ds(h * HD, HD)
        q = queries[:, cols]
        s = jnp.where(live, factor * d_out[:, cols].astype(f32), 0.0).astype(bf16)
        score = lax.dot_general(keys, q, NT, preferred_element_type=f32)
        d_prob = lax.dot_general(values, s, NT, preferred_element_type=f32)
        blocks = [score[b * TILE : (b + 1) * TILE] for b in range(BLOCKS)]
        top = jnp.max(blocks[0], axis=0, keepdims=True)
        for b in range(1, BLOCKS):
            top = jnp.maximum(
                top, jnp.where(b < n_tiles, jnp.max(blocks[b], axis=0, keepdims=True), -3e38)
            )
        expo = []
        for b in range(BLOCKS):
            shift = top if b == 0 else jnp.where(b < n_tiles, top, 1e30)
            expo.append(jnp.exp2((blocks[b] - shift) * (SCALE * LOG2E)))
        expo = jnp.concatenate(expo, 0)
        prob = expo * (1.0 / jnp.sum(expo, axis=0, keepdims=True))
        delta = jnp.sum(prob * d_prob, axis=0, keepdims=True)
        d_score = (prob * (d_prob - delta) * SCALE).astype(bf16)
        term_k = jnp.dot(d_score, q, preferred_element_type=f32)
        term_v = jnp.dot(prob.astype(bf16), s, preferred_element_type=f32)
        if h == 0:
            acc_k[...] = term_k
            acc_v[...] = term_v
        else:
            acc_k[...] += term_k
            acc_v[...] += term_v
        d_q = jnp.dot(keys_t[...], d_score, preferred_element_type=f32)
        d_queries[:, cols] = d_q.T.astype(bf16)
    both = [acc[...].reshape(PLANE, 8, HD) for acc in (acc_k, acc_v)]
    partial[...] = jnp.concatenate(both, 1).astype(bf16)


def sum_kernel(pieces, d_keys, d_values):
    _, zhs, xs, zls, cs = SIZES
    for head in range(xs * zls):
        total = None
        for zh in range(zhs):
            for c in range(cs):
                piece = pieces[(zh * xs * zls + head) * cs + c].astype(jnp.float32)
                total = piece if total is None else total + piece
        cols = pl.ds(head * HD, HD)
        d_keys[:, cols] = total[:8]
        d_values[:, cols] = total[8:]


def local(queries, keys, values, d_out, gate, tiles, text_len):
    f32, bf16 = jnp.float32, jnp.bfloat16
    block, width = keys.shape
    picked = pl.pallas_call(
        pick_kernel,
        out_shape=jax.ShapeDtypeStruct((BLOCKS, 2, block, HD), bf16),
        in_specs=[ANY, ANY],
        out_specs=ANY,
        scratch_shapes=[pltpu.SemaphoreType.DMA((BLOCKS, 2))],
        name="pick",
    )(keys, values)
    kv = lax.all_to_all(picked, ("zh", "zl"), 0, 0, axis_index_groups=GROUPS)
    image = BLOCKS * block
    d_queries, partial = pl.pallas_call(
        main_kernel,
        out_shape=(
            jax.ShapeDtypeStruct(queries.shape, bf16),
            jax.ShapeDtypeStruct((PLANE, 16, HD), bf16),
        ),
        in_specs=[SMEM, SMEM, SMEM, VMEM, VMEM, VMEM],
        out_specs=(VMEM, VMEM),
        scratch_shapes=[
            pltpu.VMEM((HD, image), bf16),
            pltpu.VMEM((image, HD), f32),
            pltpu.VMEM((image, HD), f32),
        ],
        compiler_params=pltpu.CompilerParams(vmem_limit_bytes=40 * 2**20),
        name="gradients",
    )(tiles, text_len, gate, kv, queries, d_out)
    pieces = lax.all_to_all(partial, ("zh", "x", "zl", "c"), 0, 0)
    d_keys, d_values = pl.pallas_call(
        sum_kernel,
        out_shape=(jax.ShapeDtypeStruct((8, width), f32),) * 2,
        in_specs=[VMEM],
        out_specs=(VMEM, VMEM),
        name="add_up",
    )(pieces)
    return d_queries, d_keys, d_values


def solution(mesh):
    mesh = Mesh(mesh.devices.reshape(SIZES), AXES)
    section, tensor = ("y", "zh"), ("x", "zl", "c")
    in_specs = (
        P(section, tensor),
        P(section, None),
        P(section, None),
        P(section, tensor),
        P(),
        P(),
        P(),
    )
    out_specs = (P(section, tensor), P(AXES, None), P(AXES, None))
    return jax.shard_map(local, mesh=mesh, in_specs=in_specs, out_specs=out_specs, check_vma=False)
```

```python
import jax
import jax.numpy as jnp
from jax import lax
from jax.experimental import pallas as pl
from jax.experimental.pallas import tpu as pltpu
from jax.sharding import Mesh, PartitionSpec as P

HD = 128
TILE = 128
SCALE = HD**-0.5
LOG2E = 1.4426950408889634
AXES = ("y", "zh", "x", "zl", "c")
SIZES = (8, 4, 4, 2, 2)
BLOCKS = 4
HEADS_X = 2
PLANE = 64
GROUPS = ((1, 2, 4, 7), (0, 3, 5, 6))
NT = (((1,), (1,)), ((), ()))
VMEM = pl.BlockSpec(memory_space=pltpu.VMEM)
SMEM = pl.BlockSpec(memory_space=pltpu.SMEM)
ANY = pl.BlockSpec(memory_space=pl.ANY)


def pick_kernel(keys, values, out, sems):
    x, zh, zl = lax.axis_index("x"), lax.axis_index("zh"), lax.axis_index("zl")
    first = [z % 2 for z in GROUPS[0]]
    mine = jnp.where((zh == 0) | (zh == 3), 1, 0)
    group = jnp.where(mine == zl, 0, 1)
    copies = []
    for j in range(BLOCKS):
        lo = jnp.where(group == 0, first[j], 1 - first[j])
        column = pl.ds(pl.multiple_of((x * HEADS_X + lo) * HD, HD), HD)
        for k, source in enumerate((keys, values)):
            copies.append(
                pltpu.make_async_copy(source.at[:, column], out.at[j, k], sems.at[j, k])
            )
    for copy in copies:
        copy.start()
    for copy in copies:
        copy.wait()


def main_kernel(tiles, text_len, gate, kv, queries, d_out, d_queries, partial, keys_t, acc_k, acc_v):
    f32, bf16 = jnp.float32, jnp.bfloat16
    y, zh = lax.axis_index("y"), lax.axis_index("zh")
    n_tiles, n_text = tiles[y], text_len[y]
    rows, heads = queries.shape[0], queries.shape[1] // HD
    factor = jnp.tanh(gate[...])
    keys = jnp.concatenate([kv[b, 0] for b in range(BLOCKS)], 0)
    values = jnp.concatenate([kv[b, 1] for b in range(BLOCKS)], 0)
    keys_t[...] = keys.T
    live = lax.broadcasted_iota(jnp.int32, (rows, HD), 0) + zh * rows < n_text
    for h in range(heads):
        cols = pl.ds(h * HD, HD)
        q = queries[:, cols]
        s = jnp.where(live, factor * d_out[:, cols].astype(f32), 0.0).astype(bf16)
        score = lax.dot_general(keys, q, NT, preferred_element_type=f32)
        d_prob = lax.dot_general(values, s, NT, preferred_element_type=f32)
        blocks = [score[b * TILE : (b + 1) * TILE] for b in range(BLOCKS)]
        top = jnp.max(blocks[0], axis=0, keepdims=True)
        for b in range(1, BLOCKS):
            top = jnp.maximum(
                top, jnp.where(b < n_tiles, jnp.max(blocks[b], axis=0, keepdims=True), -3e38)
            )
        expo = []
        for b in range(BLOCKS):
            shift = top if b == 0 else jnp.where(b < n_tiles, top, 1e30)
            expo.append(jnp.exp2((blocks[b] - shift) * (SCALE * LOG2E)))
        expo = jnp.concatenate(expo, 0)
        prob = expo * (1.0 / jnp.sum(expo, axis=0, keepdims=True))
        delta = jnp.sum(prob * d_prob, axis=0, keepdims=True)
        d_score = (prob * (d_prob - delta) * SCALE).astype(bf16)
        term_k = jnp.dot(d_score, q, preferred_element_type=f32)
        term_v = jnp.dot(prob.astype(bf16), s, preferred_element_type=f32)
        if h == 0:
            acc_k[...] = term_k
            acc_v[...] = term_v
        else:
            acc_k[...] += term_k
            acc_v[...] += term_v
        d_q = jnp.dot(keys_t[...], d_score, preferred_element_type=f32)
        d_queries[:, cols] = d_q.T.astype(bf16)
    both = [acc[...].reshape(PLANE, 8, HD) for acc in (acc_k, acc_v)]
    partial[...] = jnp.concatenate(both, 1).astype(bf16)


def sum_kernel(pieces, d_keys, d_values):
    _, zhs, xs, zls, cs = SIZES
    for head in range(xs * zls):
        total = None
        for zh in range(zhs):
            for c in range(cs):
                piece = pieces[(zh * xs * zls + head) * cs + c].astype(jnp.float32)
                total = piece if total is None else total + piece
        cols = pl.ds(head * HD, HD)
        d_keys[:, cols] = total[:8]
        d_values[:, cols] = total[8:]


def local(queries, keys, values, d_out, gate, tiles, text_len):
    f32, bf16 = jnp.float32, jnp.bfloat16
    block, width = keys.shape
    picked = pl.pallas_call(
        pick_kernel,
        out_shape=jax.ShapeDtypeStruct((BLOCKS, 2, block, HD), bf16),
        in_specs=[ANY, ANY],
        out_specs=VMEM,
        scratch_shapes=[pltpu.SemaphoreType.DMA((BLOCKS, 2))],
        name="pick",
    )(keys, values)
    kv = lax.all_to_all(picked, ("zh", "zl"), 0, 0, axis_index_groups=GROUPS)
    image = BLOCKS * block
    d_queries, partial = pl.pallas_call(
        main_kernel,
        out_shape=(
            jax.ShapeDtypeStruct(queries.shape, bf16),
            jax.ShapeDtypeStruct((PLANE, 16, HD), bf16),
        ),
        in_specs=[SMEM, SMEM, VMEM, VMEM, VMEM, VMEM],
        out_specs=(VMEM, VMEM),
        scratch_shapes=[
            pltpu.VMEM((HD, image), bf16),
            pltpu.VMEM((image, HD), f32),
            pltpu.VMEM((image, HD), f32),
        ],
        compiler_params=pltpu.CompilerParams(vmem_limit_bytes=40 * 2**20),
        name="gradients",
    )(tiles, text_len, gate.reshape(1, 1), kv, queries, d_out)
    pieces = lax.all_to_all(partial, ("zh", "x", "zl", "c"), 0, 0)
    d_keys, d_values = pl.pallas_call(
        sum_kernel,
        out_shape=(jax.ShapeDtypeStruct((8, width), f32),) * 2,
        in_specs=[VMEM],
        out_specs=(VMEM, VMEM),
        name="add_up",
    )(pieces)
    return d_queries, d_keys, d_values


def solution(mesh):
    mesh = Mesh(mesh.devices.reshape(SIZES), AXES)
    section, tensor = ("y", "zh"), ("x", "zl", "c")
    in_specs = (
        P(section, tensor),
        P(section, None),
        P(section, None),
        P(section, tensor),
        P(),
        P(),
        P(),
    )
    out_specs = (P(section, tensor), P(AXES, None), P(AXES, None))
    return jax.shard_map(local, mesh=mesh, in_specs=in_specs, out_specs=out_specs, check_vma=False)
```

```python
import jax
import jax.numpy as jnp
from jax import lax
from jax.experimental import pallas as pl
from jax.experimental.pallas import tpu as pltpu
from jax.sharding import Mesh, PartitionSpec as P

HD = 128
TILE = 128
SCALE = HD**-0.5
LOG2E = 1.4426950408889634
AXES = ("y", "zh", "x", "zl", "c")
SIZES = (8, 4, 4, 2, 2)
BLOCKS = 4
HEADS_X = 2
HEADS_STEP = 2
PLANE = 64
GROUPS = ((1, 2, 4, 7), (0, 3, 5, 6))
NT = (((1,), (1,)), ((), ()))
VMEM = pl.BlockSpec(memory_space=pltpu.VMEM)
SMEM = pl.BlockSpec(memory_space=pltpu.SMEM)


def pick_kernel(keys, values, out):
    x, zh, zl = lax.axis_index("x"), lax.axis_index("zh"), lax.axis_index("zl")
    first = [z % 2 for z in GROUPS[0]]
    mine = jnp.where((zh == 0) | (zh == 3), 1, 0)
    flip = jnp.where(mine == zl, 0, 1)
    for k, source in enumerate((keys, values)):
        for lo in range(2):
            head = x * HEADS_X + jnp.where(flip == 0, lo, 1 - lo)
            piece = source[:, pl.ds(pl.multiple_of(head * HD, HD), HD)]
            for j in range(BLOCKS):
                if first[j] == lo:
                    out[j, k] = piece


def main_kernel(tiles, text_len, gate, kv, queries, d_out, d_score, partial, acc_k, acc_v):
    f32, bf16 = jnp.float32, jnp.bfloat16
    y, zh = lax.axis_index("y"), lax.axis_index("zh")
    n_tiles, n_text = tiles[y], text_len[y]
    rows, heads = queries.shape[0], queries.shape[1] // HD
    steps = heads // HEADS_STEP
    factor = jnp.tanh(gate[...])
    keys = jnp.concatenate([kv[b, 0] for b in range(BLOCKS)], 0)
    values = jnp.concatenate([kv[b, 1] for b in range(BLOCKS)], 0)
    live = lax.broadcasted_iota(jnp.int32, (rows, HD), 0) + zh * rows < n_text

    def products(step):
        q, s = [], []
        for h in range(step * HEADS_STEP, (step + 1) * HEADS_STEP):
            cols = pl.ds(h * HD, HD)
            q.append(queries[:, cols])
            s.append(jnp.where(live, factor * d_out[:, cols].astype(f32), 0.0).astype(bf16))
        q, s = jnp.concatenate(q, 0), jnp.concatenate(s, 0)
        score = lax.dot_general(keys, q, NT, preferred_element_type=f32)
        d_prob = lax.dot_general(values, s, NT, preferred_element_type=f32)
        return q, s, score, d_prob

    ahead = products(0)
    for step in range(steps):
        q, s, score, d_prob = ahead
        if step < steps - 1:
            ahead = products(step + 1)
        blocks = [score[b * TILE : (b + 1) * TILE] for b in range(BLOCKS)]
        top = jnp.max(blocks[0], axis=0, keepdims=True)
        for b in range(1, BLOCKS):
            top = jnp.maximum(
                top, jnp.where(b < n_tiles, jnp.max(blocks[b], axis=0, keepdims=True), -3e38)
            )
        expo = []
        for b in range(BLOCKS):
            shift = top if b == 0 else jnp.where(b < n_tiles, top, 1e30)
            expo.append(jnp.exp2((blocks[b] - shift) * (SCALE * LOG2E)))
        expo = jnp.concatenate(expo, 0)
        inverse = 1.0 / jnp.sum(expo, axis=0, keepdims=True)
        delta = jnp.sum(expo * d_prob, axis=0, keepdims=True) * inverse
        prob = (expo * inverse).astype(bf16)
        d_s = prob * (d_prob - delta).astype(bf16)
        d_score[step] = d_s
        term_k = jnp.dot(d_s, q, preferred_element_type=f32)
        term_v = jnp.dot(prob, s, preferred_element_type=f32)
        if step == 0:
            acc_k[...] = term_k
            acc_v[...] = term_v
        else:
            acc_k[...] += term_k
            acc_v[...] += term_v
    both = [acc.reshape(PLANE, 8, HD) for acc in (acc_k[...] * SCALE, acc_v[...])]
    partial[...] = jnp.concatenate(both, 1).astype(bf16)


def query_kernel(kv, d_score, d_queries):
    keys = jnp.concatenate([kv[b, 0] for b in range(BLOCKS)], 0)
    keys_t = keys.T
    rows = d_queries.shape[0]
    for step in range(d_score.shape[0]):
        d_q = jnp.dot(keys_t, d_score[step], preferred_element_type=jnp.float32)
        d_q = (d_q * SCALE).T.astype(jnp.bfloat16)
        for i in range(HEADS_STEP):
            cols = pl.ds((step * HEADS_STEP + i) * HD, HD)
            d_queries[:, cols] = d_q[i * rows : (i + 1) * rows]


def sum_kernel(pieces, d_keys, d_values):
    _, zhs, xs, zls, cs = SIZES
    for head in range(xs * zls):
        total = None
        for zh in range(zhs):
            for c in range(cs):
                piece = pieces[(zh * xs * zls + head) * cs + c].astype(jnp.float32)
                total = piece if total is None else total + piece
        cols = pl.ds(head * HD, HD)
        d_keys[:, cols] = total[:8]
        d_values[:, cols] = total[8:]


def local(queries, keys, values, d_out, gate, tiles, text_len):
    f32, bf16 = jnp.float32, jnp.bfloat16
    block, width = keys.shape
    picked = pl.pallas_call(
        pick_kernel,
        out_shape=jax.ShapeDtypeStruct((BLOCKS, 2, block, HD), bf16),
        in_specs=[VMEM, VMEM],
        out_specs=VMEM,
        name="pick",
    )(keys, values)
    kv = lax.all_to_all(picked, ("zh", "zl"), 0, 0, axis_index_groups=GROUPS)
    image = BLOCKS * block
    rows, width_q = queries.shape
    steps = width_q // HD // HEADS_STEP
    d_score, partial = pl.pallas_call(
        main_kernel,
        out_shape=(
            jax.ShapeDtypeStruct((steps, image, rows * HEADS_STEP), bf16),
            jax.ShapeDtypeStruct((PLANE, 16, HD), bf16),
        ),
        in_specs=[SMEM, SMEM, VMEM, VMEM, VMEM, VMEM],
        out_specs=(VMEM, VMEM),
        scratch_shapes=[pltpu.VMEM((image, HD), f32), pltpu.VMEM((image, HD), f32)],
        compiler_params=pltpu.CompilerParams(vmem_limit_bytes=40 * 2**20),
        name="gradients",
    )(tiles, text_len, gate.reshape(1, 1), kv, queries, d_out)
    pieces = lax.all_to_all(partial, ("zh", "x", "zl", "c"), 0, 0)
    d_queries = pl.pallas_call(
        query_kernel,
        out_shape=jax.ShapeDtypeStruct(queries.shape, bf16),
        in_specs=[VMEM, VMEM],
        out_specs=VMEM,
        compiler_params=pltpu.CompilerParams(vmem_limit_bytes=16 * 2**20),
        cost_estimate=pl.CostEstimate(
            flops=2 * rows * width_q * image, bytes_accessed=4 * rows * width_q, transcendentals=0
        ),
        name="query_gradient",
    )(kv, d_score)
    d_keys, d_values = pl.pallas_call(
        sum_kernel,
        out_shape=(jax.ShapeDtypeStruct((8, width), f32),) * 2,
        in_specs=[VMEM],
        out_specs=(VMEM, VMEM),
        name="add_up",
    )(pieces)
    return d_queries, d_keys, d_values


def solution(mesh):
    mesh = Mesh(mesh.devices.reshape(SIZES), AXES)
    section, tensor = ("y", "zh"), ("x", "zl", "c")
    in_specs = (
        P(section, tensor),
        P(section, None),
        P(section, None),
        P(section, tensor),
        P(),
        P(),
        P(),
    )
    out_specs = (P(section, tensor), P(AXES, None), P(AXES, None))
    return jax.shard_map(local, mesh=mesh, in_specs=in_specs, out_specs=out_specs, check_vma=False)
```

```python
import jax
import jax.numpy as jnp
from jax import lax
from jax.experimental import pallas as pl
from jax.experimental.pallas import tpu as pltpu
from jax.sharding import Mesh, PartitionSpec as P

HD = 128
TILE = 128
SCALE = HD**-0.5
LOG2E = 1.4426950408889634
AXES = ("y", "zh", "x", "zl", "c")
SIZES = (8, 4, 4, 2, 2)
BLOCKS = 4
HEADS_X = 2
HEADS_STEP = 2
PLANE = 64
GROUPS = ((1, 2, 4, 7), (0, 3, 5, 6))
NT = (((1,), (1,)), ((), ()))
VMEM = pl.BlockSpec(memory_space=pltpu.VMEM)


def pick_kernel(keys, values, out):
    x, zh, zl = lax.axis_index("x"), lax.axis_index("zh"), lax.axis_index("zl")
    first = [z % 2 for z in GROUPS[0]]
    mine = jnp.where((zh == 0) | (zh == 3), 1, 0)
    flip = jnp.where(mine == zl, 0, 1)
    for k, source in enumerate((keys, values)):
        for lo in range(2):
            head = x * HEADS_X + jnp.where(flip == 0, lo, 1 - lo)
            piece = source[:, pl.ds(pl.multiple_of(head * HD, HD), HD)]
            for j in range(BLOCKS):
                if first[j] == lo:
                    out[j, k] = piece


def prepare_kernel(tiles, text_len, gate, queries, d_out, q_out, s_out, live_tiles):
    f32, bf16 = jnp.float32, jnp.bfloat16
    y, zh = lax.axis_index("y"), lax.axis_index("zh")
    picked = lax.broadcasted_iota(jnp.int32, tiles.shape, 1) == y
    n_tiles = jnp.sum(jnp.where(picked, tiles[...], 0), axis=1, keepdims=True)
    n_text = jnp.sum(jnp.where(picked, text_len[...], 0), axis=1, keepdims=True)
    live_tiles[...] = jnp.broadcast_to(n_tiles, live_tiles.shape)
    rows, heads = queries.shape[0], queries.shape[1] // HD
    factor = jnp.tanh(gate[...])
    live = lax.broadcasted_iota(jnp.int32, (rows, HD), 0) + zh * rows < n_text
    for h in range(heads):
        cols = pl.ds(h * HD, HD)
        step, place = h // HEADS_STEP, pl.ds(h % HEADS_STEP * rows, rows)
        q_out[step, place] = queries[:, cols]
        s_out[step, place] = jnp.where(live, factor * d_out[:, cols].astype(f32), 0.0).astype(bf16)


def main_kernel(live_tiles, kv, queries, scaled, d_score, partial, acc_k, acc_v):
    f32, bf16 = jnp.float32, jnp.bfloat16
    n_tiles = live_tiles[0:1, 0:1]
    steps = queries.shape[0]
    keys = jnp.concatenate([kv[b, 0] for b in range(BLOCKS)], 0)
    values = jnp.concatenate([kv[b, 1] for b in range(BLOCKS)], 0)

    def products(step):
        q, s = queries[step], scaled[step]
        score = lax.dot_general(keys, q, NT, preferred_element_type=f32)
        d_prob = lax.dot_general(values, s, NT, preferred_element_type=f32)
        return q, s, score, d_prob

    ahead = products(0)
    for step in range(steps):
        q, s, score, d_prob = ahead
        if step < steps - 1:
            ahead = products(step + 1)
        blocks = [score[b * TILE : (b + 1) * TILE] for b in range(BLOCKS)]
        top = jnp.max(blocks[0], axis=0, keepdims=True)
        for b in range(1, BLOCKS):
            top = jnp.maximum(
                top, jnp.where(b < n_tiles, jnp.max(blocks[b], axis=0, keepdims=True), -3e38)
            )
        expo = []
        for b in range(BLOCKS):
            shift = top if b == 0 else jnp.where(b < n_tiles, top, 1e30)
            expo.append(jnp.exp2((blocks[b] - shift) * (SCALE * LOG2E)))
        expo = jnp.concatenate(expo, 0)
        inverse = 1.0 / jnp.sum(expo, axis=0, keepdims=True)
        delta = jnp.sum(expo * d_prob, axis=0, keepdims=True) * inverse
        prob = (expo * inverse).astype(bf16)
        d_s = prob * (d_prob - delta).astype(bf16)
        d_score[step] = d_s
        term_k = jnp.dot(d_s, q, preferred_element_type=f32)
        term_v = jnp.dot(prob, s, preferred_element_type=f32)
        if step == 0:
            acc_k[...] = term_k
            acc_v[...] = term_v
        else:
            acc_k[...] += term_k
            acc_v[...] += term_v
    both = [acc.reshape(PLANE, 8, HD) for acc in (acc_k[...] * SCALE, acc_v[...])]
    partial[...] = jnp.concatenate(both, 1).astype(bf16)


def query_kernel(kv, d_score, d_queries):
    keys = jnp.concatenate([kv[b, 0] for b in range(BLOCKS)], 0)
    keys_t = keys.T
    rows = d_queries.shape[0]
    for step in range(d_score.shape[0]):
        d_q = jnp.dot(keys_t, d_score[step], preferred_element_type=jnp.float32)
        d_q = (d_q * SCALE).T.astype(jnp.bfloat16)
        for i in range(HEADS_STEP):
            cols = pl.ds((step * HEADS_STEP + i) * HD, HD)
            d_queries[:, cols] = d_q[i * rows : (i + 1) * rows]


def sum_kernel(pieces, d_keys, d_values):
    _, zhs, xs, zls, cs = SIZES
    for head in range(xs * zls):
        total = None
        for zh in range(zhs):
            for c in range(cs):
                piece = pieces[(zh * xs * zls + head) * cs + c].astype(jnp.float32)
                total = piece if total is None else total + piece
        cols = pl.ds(head * HD, HD)
        d_keys[:, cols] = total[:8]
        d_values[:, cols] = total[8:]


def in_vmem(array):
    return pltpu.with_memory_space_constraint(array, pltpu.VMEM)


def local(queries, keys, values, d_out, gate, tiles, text_len):
    f32, bf16 = jnp.float32, jnp.bfloat16
    block, width = keys.shape
    rows, width_q = queries.shape
    steps = width_q // HD // HEADS_STEP
    image = BLOCKS * block
    picked = pl.pallas_call(
        pick_kernel,
        out_shape=pltpu.VMEM((BLOCKS, 2, block, HD), bf16),
        in_specs=[VMEM, VMEM],
        out_specs=VMEM,
        name="pick",
    )(keys, values)
    kv = in_vmem(lax.all_to_all(picked, ("zh", "zl"), 0, 0, axis_index_groups=GROUPS))
    by_step = (steps, rows * HEADS_STEP, HD)
    q, scaled, live_tiles = pl.pallas_call(
        prepare_kernel,
        out_shape=(
            pltpu.VMEM(by_step, bf16),
            pltpu.VMEM(by_step, bf16),
            pltpu.VMEM((8, HD), jnp.int32),
        ),
        in_specs=[VMEM] * 5,
        out_specs=(VMEM,) * 3,
        compiler_params=pltpu.CompilerParams(vmem_limit_bytes=16 * 2**20),
        cost_estimate=pl.CostEstimate(
            flops=4 * rows * width_q, bytes_accessed=8 * rows * width_q, transcendentals=0
        ),
        name="prepare",
    )(tiles.reshape(1, -1), text_len.reshape(1, -1), gate.reshape(1, 1), queries, d_out)
    d_score, partial = pl.pallas_call(
        main_kernel,
        out_shape=(
            pltpu.VMEM((steps, image, rows * HEADS_STEP), bf16),
            pltpu.VMEM((PLANE, 16, HD), bf16),
        ),
        in_specs=[VMEM] * 4,
        out_specs=(VMEM, VMEM),
        scratch_shapes=[pltpu.VMEM((image, HD), f32), pltpu.VMEM((image, HD), f32)],
        compiler_params=pltpu.CompilerParams(vmem_limit_bytes=40 * 2**20),
        name="gradients",
    )(in_vmem(live_tiles), kv, in_vmem(q), in_vmem(scaled))
    pieces = lax.all_to_all(partial, ("zh", "x", "zl", "c"), 0, 0)
    d_queries = pl.pallas_call(
        query_kernel,
        out_shape=jax.ShapeDtypeStruct(queries.shape, bf16),
        in_specs=[VMEM, VMEM],
        out_specs=VMEM,
        compiler_params=pltpu.CompilerParams(vmem_limit_bytes=16 * 2**20),
        cost_estimate=pl.CostEstimate(
            flops=2 * rows * width_q * image, bytes_accessed=4 * rows * width_q, transcendentals=0
        ),
        name="query_gradient",
    )(kv, in_vmem(d_score))
    d_keys, d_values = pl.pallas_call(
        sum_kernel,
        out_shape=(jax.ShapeDtypeStruct((8, width), f32),) * 2,
        in_specs=[VMEM],
        out_specs=(VMEM, VMEM),
        name="add_up",
    )(in_vmem(pieces))
    return d_queries, d_keys, d_values


def solution(mesh):
    mesh = Mesh(mesh.devices.reshape(SIZES), AXES)
    section, tensor = ("y", "zh"), ("x", "zl", "c")
    in_specs = (
        P(section, tensor),
        P(section, None),
        P(section, None),
        P(section, tensor),
        P(),
        P(),
        P(),
    )
    out_specs = (P(section, tensor), P(AXES, None), P(AXES, None))
    return jax.shard_map(local, mesh=mesh, in_specs=in_specs, out_specs=out_specs, check_vma=False)
```

```python
import jax
import jax.numpy as jnp
from jax import lax
from jax.experimental import pallas as pl
from jax.experimental.pallas import tpu as pltpu
from jax.sharding import Mesh, PartitionSpec as P

HD = 128
TILE = 128
SCALE = HD**-0.5
LOG2E = 1.4426950408889634
AXES = ("y", "zh", "x", "zl", "c")
SIZES = (8, 4, 4, 2, 2)
BLOCKS = 4
HEADS_X = 2
HEADS_STEP = 2
PLANE = 64
GROUPS = ((1, 2, 4, 7), (0, 3, 5, 6))
NT = (((1,), (1,)), ((), ()))
VMEM = pl.BlockSpec(memory_space=pltpu.VMEM)
HBM = pl.BlockSpec(memory_space=pltpu.HBM)


def partner(zh, c):
    return lax.bitwise_xor(zh, 2 + c)


def end_of(zh):
    return jnp.where((zh == 0) | (zh == BLOCKS - 1), 1, 0)


def pick_kernel(keys, values, own, first, second, blocks, sems):
    x, zh, zl, c = (lax.axis_index(axis) for axis in ("x", "zh", "zl", "c"))
    copies = [
        pltpu.make_async_copy(source, blocks.at[k], sems.at[k])
        for k, source in enumerate((keys, values))
    ]
    for copy in copies:
        copy.start()
    flip = lax.rem(end_of(zh) + zl, 2)
    for k in range(2):
        copies[k].wait()
        for section, out in ((zh, own), (partner(zh, c), first), (lax.bitwise_xor(zh, 1), second)):
            head = x * HEADS_X + lax.rem(end_of(section) + flip, 2)
            out[k] = blocks[k, :, pl.ds(pl.multiple_of(head * HD, HD), HD)]


def prepare_kernel(
    tiles, text_len, queries, d_out, q_out, d_live, live_tiles, s_tiles, s_text, q, d, sems
):
    pairs = ((d_out, d), (queries, q), (text_len, s_text), (tiles, s_tiles))
    copies = [pltpu.make_async_copy(*pair, sems.at[i]) for i, pair in enumerate(pairs)]
    for copy in copies:
        copy.start()
    for copy in copies:
        copy.wait()
    y, zh = lax.axis_index("y"), lax.axis_index("zh")
    live_tiles[...] = jnp.full(live_tiles.shape, s_tiles[y], jnp.int32)
    rows, heads = queries.shape[0], queries.shape[1] // HD
    live = lax.broadcasted_iota(jnp.int32, (rows, HD), 0) + zh * rows < s_text[y]
    for h in range(heads):
        cols = pl.ds(h * HD, HD)
        step, place = h // HEADS_STEP, pl.ds(h % HEADS_STEP * rows, rows)
        q_out[step, place] = q[:, cols]
        d_live[step, place] = jnp.where(live, d[:, cols].astype(jnp.float32), 0.0).astype(jnp.bfloat16)


def stacked(parts, k):
    return jnp.concatenate([part[k] for part in parts], 0)


def products(parts, q, s):
    score = lax.dot_general(stacked(parts, 0), q, NT, preferred_element_type=jnp.float32)
    d_prob = lax.dot_general(stacked(parts, 1), s, NT, preferred_element_type=jnp.float32)
    return score, d_prob


def largest(score, live):
    top = -3e38
    for b in range(len(live)):
        part = jnp.max(score[b * TILE : (b + 1) * TILE], axis=0, keepdims=True)
        top = jnp.maximum(top, jnp.where(live[b], part, -3e38))
    return top


def exponentials(score, top, live):
    parts = []
    for b in range(len(live)):
        shift = jnp.where(live[b], top, 1e30)
        parts.append(jnp.exp2((score[b * TILE : (b + 1) * TILE] - shift) * (SCALE * LOG2E)))
    return jnp.concatenate(parts, 0)


def places():
    zh, c = lax.axis_index("zh"), lax.axis_index("c")
    return zh, partner(zh, c), lax.bitwise_xor(zh, 1), partner(zh, 1 - c)


def first_kernel(live_tiles, kv_0, kv_1, queries, d_out, expo_out, d_prob_out, stats):
    live = [place < live_tiles[0:1, 0:1] for place in places()[:2]]
    kv = (kv_0, kv_1)
    steps = queries.shape[0]
    ahead = products(kv, queries[0], d_out[0])
    for step in range(steps):
        score, d_prob = ahead
        if step < steps - 1:
            ahead = products(kv, queries[step + 1], d_out[step + 1])
        top = largest(score, live)
        expo = exponentials(score, top, live)
        expo_out[step] = expo
        d_prob_out[step] = d_prob
        stats[step, 0:1] = top
        stats[step, 1:2] = jnp.sum(expo, axis=0, keepdims=True)
        stats[step, 2:3] = jnp.sum(expo * d_prob, axis=0, keepdims=True)


def main_kernel(
    live_tiles, expo_1, d_prob_1, stats, kv_2, kv_3, queries, d_out, d_score, partial, acc_k, acc_v
):
    f32, bf16 = jnp.float32, jnp.bfloat16
    live = [place < live_tiles[0:1, 0:1] for place in places()[2:]]
    kv = (kv_2, kv_3)
    steps, half = queries.shape[0], expo_1.shape[1]
    ahead = products(kv, queries[0], d_out[0])
    for step in range(steps):
        q, s = queries[step], d_out[step]
        score, d_prob = ahead
        if step < steps - 1:
            ahead = products(kv, queries[step + 1], d_out[step + 1])
        top_1, sum_1, dot_1 = (stats[step, i : i + 1] for i in range(3))
        top = jnp.maximum(top_1, largest(score, live))
        expo = exponentials(score, top, live)
        weight = jnp.exp2((top_1 - top) * (SCALE * LOG2E))
        inverse = 1.0 / (sum_1 * weight + jnp.sum(expo, axis=0, keepdims=True))
        delta = (dot_1 * weight + jnp.sum(expo * d_prob, axis=0, keepdims=True)) * inverse
        prob_1 = (expo_1[step] * (weight * inverse)).astype(bf16)
        prob_2 = (expo * inverse).astype(bf16)
        d_s_1 = prob_1 * (d_prob_1[step] - delta).astype(bf16)
        d_s_2 = prob_2 * (d_prob - delta).astype(bf16)
        d_score[step, :half] = d_s_1
        d_score[step, half:] = d_s_2
        term_k = jnp.dot(jnp.concatenate([d_s_1, d_s_2], 0), q, preferred_element_type=f32)
        term_v = jnp.dot(jnp.concatenate([prob_1, prob_2], 0), s, preferred_element_type=f32)
        if step == 0:
            acc_k[...] = term_k
            acc_v[...] = term_v
        else:
            acc_k[...] += term_k
            acc_v[...] += term_v
    both = [acc.reshape(PLANE, 8, HD) for acc in (acc_k[...], acc_v[...])]
    both = jnp.concatenate(both, 1).astype(bf16)
    run = PLANE // BLOCKS
    for b, place in enumerate(places()):
        partial[pl.ds(place * run, run)] = both[b * run : (b + 1) * run]


def query_kernel(gate, kv_0, kv_1, kv_2, kv_3, d_score, d_queries):
    factor = jnp.tanh(gate[...]) * SCALE
    keys_t = stacked((kv_0, kv_1, kv_2, kv_3), 0).T
    rows = d_queries.shape[0]
    for step in range(d_score.shape[0]):
        d_q = jnp.dot(keys_t, d_score[step], preferred_element_type=jnp.float32)
        d_q = (d_q * factor).T.astype(jnp.bfloat16)
        for i in range(HEADS_STEP):
            cols = pl.ds((step * HEADS_STEP + i) * HD, HD)
            d_queries[:, cols] = d_q[i * rows : (i + 1) * rows]


def sum_kernel(gate, pieces, d_keys, d_values):
    factor = jnp.tanh(gate[...])
    _, zhs, xs, zls, cs = SIZES
    for head in range(xs * zls):
        total = None
        for zh in range(zhs):
            for c in range(cs):
                piece = pieces[(zh * xs * zls + head) * cs + c].astype(jnp.float32)
                total = piece if total is None else total + piece
        cols = pl.ds(head * HD, HD)
        d_keys[:, cols] = total[:8] * (factor * SCALE)
        d_values[:, cols] = total[8:] * factor


def in_vmem(array):
    return pltpu.with_memory_space_constraint(array, pltpu.VMEM)


def in_hbm(array):
    return pltpu.with_memory_space_constraint(array, pltpu.HBM)


def swap(value, step):
    pairs = []
    for c in range(2):
        for group in GROUPS:
            pairs += [(2 * group[i] + c, 2 * group[i ^ step[c]] + c) for i in range(BLOCKS)]
    return in_vmem(lax.ppermute(value, ("zh", "zl", "c"), pairs))


def local(queries, keys, values, d_out, gate, tiles, text_len):
    f32, bf16 = jnp.float32, jnp.bfloat16
    gate = gate.reshape(1, 1)
    block, width = keys.shape
    rows, width_q = queries.shape
    steps = width_q // HD // HEADS_STEP
    image = BLOCKS * block
    own, first, second = pl.pallas_call(
        pick_kernel,
        out_shape=(pltpu.VMEM((2, block, HD), bf16),) * 3,
        in_specs=[HBM, HBM],
        out_specs=(VMEM,) * 3,
        scratch_shapes=[pltpu.VMEM((2, block, width), bf16), pltpu.SemaphoreType.DMA((2,))],
        name="pick",
    )(in_hbm(keys), in_hbm(values))
    kv_0, kv_1, kv_2 = in_vmem(own), swap(first, (2, 3)), swap(second, (1, 1))
    kv_3 = in_vmem(lax.ppermute(kv_1, "c", [(0, 1), (1, 0)]))
    by_step = (steps, rows * HEADS_STEP, HD)
    q, d_live, live_tiles = pl.pallas_call(
        prepare_kernel,
        out_shape=(
            pltpu.VMEM(by_step, bf16),
            pltpu.VMEM(by_step, bf16),
            pltpu.VMEM((8, HD), jnp.int32),
        ),
        in_specs=[HBM] * 4,
        out_specs=(VMEM,) * 3,
        scratch_shapes=[
            pltpu.SMEM(tiles.shape, jnp.int32),
            pltpu.SMEM(text_len.shape, jnp.int32),
            pltpu.VMEM(queries.shape, bf16),
            pltpu.VMEM(queries.shape, bf16),
            pltpu.SemaphoreType.DMA((4,)),
        ],
        compiler_params=pltpu.CompilerParams(vmem_limit_bytes=16 * 2**20),
        cost_estimate=pl.CostEstimate(
            flops=4 * rows * width_q, bytes_accessed=8 * rows * width_q, transcendentals=0
        ),
        name="prepare",
    )(*(in_hbm(array) for array in (tiles, text_len, queries, d_out)))
    q, d_live, live_tiles = in_vmem(q), in_vmem(d_live), in_vmem(live_tiles)
    by_half = (steps, image // 2, rows * HEADS_STEP)
    expo, d_prob, stats = pl.pallas_call(
        first_kernel,
        out_shape=(
            pltpu.VMEM(by_half, f32),
            pltpu.VMEM(by_half, f32),
            pltpu.VMEM((steps, 8, rows * HEADS_STEP), f32),
        ),
        in_specs=[VMEM] * 5,
        out_specs=(VMEM,) * 3,
        compiler_params=pltpu.CompilerParams(vmem_limit_bytes=24 * 2**20),
        cost_estimate=pl.CostEstimate(
            flops=40 * rows * width_q * image, bytes_accessed=rows * width_q, transcendentals=0
        ),
        name="first_half",
    )(live_tiles, kv_0, kv_1, q, d_live)
    d_score, partial = pl.pallas_call(
        main_kernel,
        out_shape=(
            pltpu.VMEM((steps, image, rows * HEADS_STEP), bf16),
            pltpu.VMEM((PLANE, 16, HD), bf16),
        ),
        in_specs=[VMEM] * 8,
        out_specs=(VMEM, VMEM),
        scratch_shapes=[pltpu.VMEM((image, HD), f32), pltpu.VMEM((image, HD), f32)],
        compiler_params=pltpu.CompilerParams(vmem_limit_bytes=36 * 2**20),
        name="gradients",
    )(live_tiles, in_vmem(expo), in_vmem(d_prob), in_vmem(stats), kv_2, kv_3, q, d_live)
    pieces = lax.all_to_all(partial, ("zh", "x", "zl", "c"), 0, 0)
    d_queries = pl.pallas_call(
        query_kernel,
        out_shape=jax.ShapeDtypeStruct(queries.shape, bf16),
        in_specs=[VMEM] * 6,
        out_specs=VMEM,
        compiler_params=pltpu.CompilerParams(vmem_limit_bytes=16 * 2**20),
        cost_estimate=pl.CostEstimate(
            flops=2 * rows * width_q * image, bytes_accessed=4 * rows * width_q, transcendentals=0
        ),
        name="query_gradient",
    )(gate, kv_0, kv_1, kv_2, kv_3, in_vmem(d_score))
    d_keys, d_values = pl.pallas_call(
        sum_kernel,
        out_shape=(jax.ShapeDtypeStruct((8, width), f32),) * 2,
        in_specs=[VMEM, VMEM],
        out_specs=(VMEM, VMEM),
        name="add_up",
    )(gate, in_vmem(pieces))
    return d_queries, d_keys, d_values


def solution(mesh):
    mesh = Mesh(mesh.devices.reshape(SIZES), AXES)
    section, tensor = ("y", "zh"), ("x", "zl", "c")
    in_specs = (
        P(section, tensor),
        P(section, None),
        P(section, None),
        P(section, tensor),
        P(),
        P(),
        P(),
    )
    out_specs = (P(section, tensor), P(AXES, None), P(AXES, None))
    return jax.shard_map(local, mesh=mesh, in_specs=in_specs, out_specs=out_specs, check_vma=False)
```

```python
import jax
import jax.numpy as jnp
from jax import lax
from jax.experimental import pallas as pl
from jax.experimental.pallas import tpu as pltpu
from jax.sharding import Mesh, PartitionSpec as P

HD = 128
TILE = 128
SCALE = HD**-0.5
LOG2E = 1.4426950408889634
AXES = ("y", "zh", "x", "zl", "c")
SIZES = (8, 4, 4, 2, 2)
BLOCKS = 4
HEADS_X = 2
HEADS_STEP = 2
PLANE = 64
GROUPS = ((1, 2, 4, 7), (0, 3, 5, 6))
FIRST_ZH, FIRST_X = 2, 2
NT = (((1,), (1,)), ((), ()))
VMEM = pl.BlockSpec(memory_space=pltpu.VMEM)
HBM = pl.BlockSpec(memory_space=pltpu.HBM)


def partner(zh, c):
    return lax.bitwise_xor(zh, 2 + c)


def end_of(zh):
    return jnp.where((zh == 0) | (zh == BLOCKS - 1), 1, 0)


def pick_kernel(keys, values, own, first, second, blocks, sems):
    x, zh, zl, c = (lax.axis_index(axis) for axis in ("x", "zh", "zl", "c"))
    copies = [
        pltpu.make_async_copy(source, blocks.at[k], sems.at[k])
        for k, source in enumerate((keys, values))
    ]
    for copy in copies:
        copy.start()
    flip = lax.rem(end_of(zh) + zl, 2)
    for k in range(2):
        copies[k].wait()
        for section, out in ((zh, own), (partner(zh, c), first), (lax.bitwise_xor(zh, 1), second)):
            head = x * HEADS_X + lax.rem(end_of(section) + flip, 2)
            out[k] = blocks[k, :, pl.ds(pl.multiple_of(head * HD, HD), HD)]


def prepare_kernel(
    tiles, text_len, queries, d_out, q_out, d_live, live_tiles, s_tiles, s_text, q, d, sems
):
    pairs = ((d_out, d), (queries, q), (text_len, s_text), (tiles, s_tiles))
    copies = [pltpu.make_async_copy(*pair, sems.at[i]) for i, pair in enumerate(pairs)]
    for copy in copies:
        copy.start()
    for copy in copies:
        copy.wait()
    y, zh = lax.axis_index("y"), lax.axis_index("zh")
    live_tiles[...] = jnp.full(live_tiles.shape, s_tiles[y], jnp.int32)
    rows, heads = queries.shape[0], queries.shape[1] // HD
    live = lax.broadcasted_iota(jnp.int32, (rows, HD), 0) + zh * rows < s_text[y]
    for h in range(heads):
        cols = pl.ds(h * HD, HD)
        step, place = h // HEADS_STEP, pl.ds(h % HEADS_STEP * rows, rows)
        q_out[step, place] = q[:, cols]
        d_live[step, place] = jnp.where(live, d[:, cols].astype(jnp.float32), 0.0).astype(jnp.bfloat16)


def stacked(parts, k):
    return jnp.concatenate([part[k] for part in parts], 0)


def products(parts, q, s):
    score = lax.dot_general(stacked(parts, 0), q, NT, preferred_element_type=jnp.float32)
    d_prob = lax.dot_general(stacked(parts, 1), s, NT, preferred_element_type=jnp.float32)
    return score, d_prob


def largest(score, live):
    top = -3e38
    for b in range(len(live)):
        part = jnp.max(score[b * TILE : (b + 1) * TILE], axis=0, keepdims=True)
        top = jnp.maximum(top, jnp.where(live[b], part, -3e38))
    return top


def exponentials(score, top, live):
    parts = []
    for b in range(len(live)):
        shift = jnp.where(live[b], top, 1e30)
        parts.append(jnp.exp2((score[b * TILE : (b + 1) * TILE] - shift) * (SCALE * LOG2E)))
    return jnp.concatenate(parts, 0)


def places():
    zh, c = lax.axis_index("zh"), lax.axis_index("c")
    return zh, partner(zh, c), lax.bitwise_xor(zh, 1), partner(zh, 1 - c)


def first_kernel(live_tiles, kv_0, kv_1, kv_2, queries, d_out, expo_out, d_prob_out, stats):
    live = [place < live_tiles[0:1, 0:1] for place in places()[:3]]
    kv = (kv_0, kv_1, kv_2)
    steps = queries.shape[0]
    ahead = products(kv, queries[0], d_out[0])
    for step in range(steps):
        score, d_prob = ahead
        if step < steps - 1:
            ahead = products(kv, queries[step + 1], d_out[step + 1])
        top = largest(score, live)
        expo = exponentials(score, top, live)
        expo_out[step] = expo
        d_prob_out[step] = d_prob
        stats[step, 0:1] = top
        stats[step, 1:2] = jnp.sum(expo, axis=0, keepdims=True)
        stats[step, 2:3] = jnp.sum(expo * d_prob, axis=0, keepdims=True)


def main_kernel(
    live_tiles, expo_1, d_prob_1, stats, kv_3, queries, d_out, d_score, partial, acc_k, acc_v
):
    f32, bf16 = jnp.float32, jnp.bfloat16
    live = [place < live_tiles[0:1, 0:1] for place in places()[3:]]
    kv = (kv_3,)
    steps, before = queries.shape[0], expo_1.shape[1]
    ahead = products(kv, queries[0], d_out[0])
    for step in range(steps):
        q, s = queries[step], d_out[step]
        score, d_prob = ahead
        if step < steps - 1:
            ahead = products(kv, queries[step + 1], d_out[step + 1])
        top_1, sum_1, dot_1 = (stats[step, i : i + 1] for i in range(3))
        top = jnp.maximum(top_1, largest(score, live))
        expo = exponentials(score, top, live)
        weight = jnp.exp2((top_1 - top) * (SCALE * LOG2E))
        inverse = 1.0 / (sum_1 * weight + jnp.sum(expo, axis=0, keepdims=True))
        delta = (dot_1 * weight + jnp.sum(expo * d_prob, axis=0, keepdims=True)) * inverse
        prob_1 = (expo_1[step] * (weight * inverse)).astype(bf16)
        prob_2 = (expo * inverse).astype(bf16)
        d_s_1 = prob_1 * (d_prob_1[step] - delta).astype(bf16)
        d_s_2 = prob_2 * (d_prob - delta).astype(bf16)
        d_score[step, :before] = d_s_1
        d_score[step, before:] = d_s_2
        term_k = jnp.dot(jnp.concatenate([d_s_1, d_s_2], 0), q, preferred_element_type=f32)
        term_v = jnp.dot(jnp.concatenate([prob_1, prob_2], 0), s, preferred_element_type=f32)
        if step == 0:
            acc_k[...] = term_k
            acc_v[...] = term_v
        else:
            acc_k[...] += term_k
            acc_v[...] += term_v
    both = [acc.reshape(PLANE, 8, HD) for acc in (acc_k[...], acc_v[...])]
    both = jnp.concatenate(both, 1).astype(bf16)
    run = PLANE // BLOCKS
    part = run // SIZES[2]
    for b, place in enumerate(places()):
        for x in range(SIZES[2]):
            at = lax.bitwise_xor(place, FIRST_ZH) * run + (x ^ FIRST_X) * part
            partial[pl.ds(at, part)] = both[b * run + x * part : b * run + (x + 1) * part]


def query_kernel(gate, kv_0, kv_1, kv_2, kv_3, d_score, d_queries):
    factor = jnp.tanh(gate[...]) * SCALE
    keys_t = stacked((kv_0, kv_1, kv_2, kv_3), 0).T
    rows = d_queries.shape[0]
    for step in range(d_score.shape[0]):
        d_q = jnp.dot(keys_t, d_score[step], preferred_element_type=jnp.float32)
        d_q = (d_q * factor).T.astype(jnp.bfloat16)
        for i in range(HEADS_STEP):
            cols = pl.ds((step * HEADS_STEP + i) * HD, HD)
            d_queries[:, cols] = d_q[i * rows : (i + 1) * rows]


def sum_kernel(gate, pieces, d_keys, d_values):
    factor = jnp.tanh(gate[...])
    _, zhs, xs, zls, cs = SIZES
    for head in range(xs * zls):
        place = ((head // zls) ^ FIRST_X) * zls + head % zls
        total = None
        for zh in range(zhs):
            for c in range(cs):
                piece = pieces[(zh * xs * zls + place) * cs + c].astype(jnp.float32)
                total = piece if total is None else total + piece
        cols = pl.ds(head * HD, HD)
        d_keys[:, cols] = total[:8] * (factor * SCALE)
        d_values[:, cols] = total[8:] * factor


def in_vmem(array):
    return pltpu.with_memory_space_constraint(array, pltpu.VMEM)


def in_hbm(array):
    return pltpu.with_memory_space_constraint(array, pltpu.HBM)


def swap(value, step):
    pairs = []
    for c in range(2):
        for group in GROUPS:
            pairs += [(2 * group[i] + c, 2 * group[i ^ step[c]] + c) for i in range(BLOCKS)]
    return in_vmem(lax.ppermute(value, ("zh", "zl", "c"), pairs))


def local(queries, keys, values, d_out, gate, tiles, text_len):
    f32, bf16 = jnp.float32, jnp.bfloat16
    gate = gate.reshape(1, 1)
    block, width = keys.shape
    rows, width_q = queries.shape
    steps = width_q // HD // HEADS_STEP
    image = BLOCKS * block
    own, first, second = pl.pallas_call(
        pick_kernel,
        out_shape=(pltpu.VMEM((2, block, HD), bf16),) * 3,
        in_specs=[HBM, HBM],
        out_specs=(VMEM,) * 3,
        scratch_shapes=[pltpu.VMEM((2, block, width), bf16), pltpu.SemaphoreType.DMA((2,))],
        name="pick",
    )(in_hbm(keys), in_hbm(values))
    kv_0, kv_1, kv_2 = in_vmem(own), swap(first, (2, 3)), swap(second, (1, 1))
    kv_3 = in_vmem(lax.ppermute(kv_1, "c", [(0, 1), (1, 0)]))
    by_step = (steps, rows * HEADS_STEP, HD)
    q, d_live, live_tiles = pl.pallas_call(
        prepare_kernel,
        out_shape=(
            pltpu.VMEM(by_step, bf16),
            pltpu.VMEM(by_step, bf16),
            pltpu.VMEM((8, HD), jnp.int32),
        ),
        in_specs=[HBM] * 4,
        out_specs=(VMEM,) * 3,
        scratch_shapes=[
            pltpu.SMEM(tiles.shape, jnp.int32),
            pltpu.SMEM(text_len.shape, jnp.int32),
            pltpu.VMEM(queries.shape, bf16),
            pltpu.VMEM(queries.shape, bf16),
            pltpu.SemaphoreType.DMA((4,)),
        ],
        compiler_params=pltpu.CompilerParams(vmem_limit_bytes=16 * 2**20),
        cost_estimate=pl.CostEstimate(
            flops=4 * rows * width_q, bytes_accessed=8 * rows * width_q, transcendentals=0
        ),
        name="prepare",
    )(*(in_hbm(array) for array in (tiles, text_len, queries, d_out)))
    q, d_live, live_tiles = in_vmem(q), in_vmem(d_live), in_vmem(live_tiles)
    by_part = (steps, image - block, rows * HEADS_STEP)
    expo, d_prob, stats = pl.pallas_call(
        first_kernel,
        out_shape=(
            pltpu.VMEM(by_part, f32),
            pltpu.VMEM(by_part, f32),
            pltpu.VMEM((steps, 8, rows * HEADS_STEP), f32),
        ),
        in_specs=[VMEM] * 6,
        out_specs=(VMEM,) * 3,
        compiler_params=pltpu.CompilerParams(vmem_limit_bytes=24 * 2**20),
        cost_estimate=pl.CostEstimate(
            flops=40 * rows * width_q * image, bytes_accessed=rows * width_q, transcendentals=0
        ),
        name="three_blocks",
    )(live_tiles, kv_0, kv_1, kv_2, q, d_live)
    d_score, partial = pl.pallas_call(
        main_kernel,
        out_shape=(
            pltpu.VMEM((steps, image, rows * HEADS_STEP), bf16),
            pltpu.VMEM((PLANE, 16, HD), bf16),
        ),
        in_specs=[VMEM] * 7,
        out_specs=(VMEM, VMEM),
        scratch_shapes=[pltpu.VMEM((image, HD), f32), pltpu.VMEM((image, HD), f32)],
        compiler_params=pltpu.CompilerParams(vmem_limit_bytes=36 * 2**20),
        name="gradients",
    )(live_tiles, in_vmem(expo), in_vmem(d_prob), in_vmem(stats), kv_3, q, d_live)
    _, zhs, xs, zls, cs = SIZES
    members = [
        ((zh ^ FIRST_ZH) * xs + (x ^ FIRST_X)) * zls * cs + i
        for zh in range(zhs)
        for x in range(xs)
        for i in range(zls * cs)
    ]
    pieces = lax.all_to_all(partial, ("zh", "x", "zl", "c"), 0, 0, axis_index_groups=[members])
    d_queries = pl.pallas_call(
        query_kernel,
        out_shape=jax.ShapeDtypeStruct(queries.shape, bf16),
        in_specs=[VMEM] * 6,
        out_specs=VMEM,
        compiler_params=pltpu.CompilerParams(vmem_limit_bytes=16 * 2**20),
        cost_estimate=pl.CostEstimate(
            flops=2 * rows * width_q * image, bytes_accessed=4 * rows * width_q, transcendentals=0
        ),
        name="query_gradient",
    )(gate, kv_0, kv_1, kv_2, kv_3, in_vmem(d_score))
    d_keys, d_values = pl.pallas_call(
        sum_kernel,
        out_shape=(jax.ShapeDtypeStruct((8, width), f32),) * 2,
        in_specs=[VMEM, VMEM],
        out_specs=(VMEM, VMEM),
        name="add_up",
    )(gate, in_vmem(pieces))
    return d_queries, d_keys, d_values


def solution(mesh):
    mesh = Mesh(mesh.devices.reshape(SIZES), AXES)
    section, tensor = ("y", "zh"), ("x", "zl", "c")
    in_specs = (
        P(section, tensor),
        P(section, None),
        P(section, None),
        P(section, tensor),
        P(),
        P(),
        P(),
    )
    out_specs = (P(section, tensor), P(AXES, None), P(AXES, None))
    return jax.shard_map(local, mesh=mesh, in_specs=in_specs, out_specs=out_specs, check_vma=False)
```

```python
import jax
import jax.numpy as jnp
from jax import lax
from jax.experimental import pallas as pl
from jax.experimental.pallas import tpu as pltpu
from jax.sharding import Mesh, PartitionSpec as P

HD = 128
TILE = 128
SCALE = HD**-0.5
LOG2E = 1.4426950408889634
AXES = ("y", "zh", "x", "zl", "c")
SIZES = (8, 4, 4, 2, 2)
BLOCKS = 4
HEADS_X = 2
HEADS_STEP = 2
PLANE = 64
GROUPS = ((1, 2, 4, 7), (0, 3, 5, 6))
FIRST_ZH, FIRST_IN = 2, 9
NT = (((1,), (1,)), ((), ()))
VMEM = pl.BlockSpec(memory_space=pltpu.VMEM)
HBM = pl.BlockSpec(memory_space=pltpu.HBM)


def partner(zh, c):
    return lax.bitwise_xor(zh, 2 + c)


def end_of(zh):
    return jnp.where((zh == 0) | (zh == BLOCKS - 1), 1, 0)


def pick_kernel(keys, values, own, first, second, blocks, sems):
    x, zh, zl, c = (lax.axis_index(axis) for axis in ("x", "zh", "zl", "c"))
    copies = [
        pltpu.make_async_copy(source, blocks.at[k], sems.at[k])
        for k, source in enumerate((keys, values))
    ]
    for copy in copies:
        copy.start()
    flip = lax.rem(end_of(zh) + zl, 2)
    for k in range(2):
        copies[k].wait()
        for section, out in ((zh, own), (partner(zh, c), first), (lax.bitwise_xor(zh, 1), second)):
            head = x * HEADS_X + lax.rem(end_of(section) + flip, 2)
            out[k] = blocks[k, :, pl.ds(pl.multiple_of(head * HD, HD), HD)]


def prepare_kernel(
    tiles, text_len, queries, d_out, q_out, d_live, live_tiles, s_tiles, s_text, q, d, sems
):
    pairs = ((d_out, d), (queries, q), (text_len, s_text), (tiles, s_tiles))
    copies = [pltpu.make_async_copy(*pair, sems.at[i]) for i, pair in enumerate(pairs)]
    for copy in copies:
        copy.start()
    for copy in copies:
        copy.wait()
    y, zh = lax.axis_index("y"), lax.axis_index("zh")
    live_tiles[...] = jnp.full(live_tiles.shape, s_tiles[y], jnp.int32)
    rows, heads = queries.shape[0], queries.shape[1] // HD
    live = lax.broadcasted_iota(jnp.int32, (rows, HD), 0) + zh * rows < s_text[y]
    for h in range(heads):
        cols = pl.ds(h * HD, HD)
        step, place = h // HEADS_STEP, pl.ds(h % HEADS_STEP * rows, rows)
        q_out[step, place] = q[:, cols]
        d_live[step, place] = jnp.where(live, d[:, cols].astype(jnp.float32), 0.0).astype(jnp.bfloat16)


def stacked(parts, k):
    return jnp.concatenate([part[k] for part in parts], 0)


def products(parts, q, s):
    score = lax.dot_general(stacked(parts, 0), q, NT, preferred_element_type=jnp.float32)
    d_prob = lax.dot_general(stacked(parts, 1), s, NT, preferred_element_type=jnp.float32)
    return score, d_prob


def largest(score, live):
    top = -3e38
    for b in range(len(live)):
        part = jnp.max(score[b * TILE : (b + 1) * TILE], axis=0, keepdims=True)
        top = jnp.maximum(top, jnp.where(live[b], part, -3e38))
    return top


def exponentials(score, top, live):
    parts = []
    for b in range(len(live)):
        shift = jnp.where(live[b], top, 1e30)
        parts.append(jnp.exp2((score[b * TILE : (b + 1) * TILE] - shift) * (SCALE * LOG2E)))
    return jnp.concatenate(parts, 0)


def places():
    zh, c = lax.axis_index("zh"), lax.axis_index("c")
    return zh, partner(zh, c), lax.bitwise_xor(zh, 1), partner(zh, 1 - c)


def first_kernel(live_tiles, kv_0, kv_1, kv_2, queries, d_out, expo_out, d_prob_out, stats):
    live = [place < live_tiles[0:1, 0:1] for place in places()[:3]]
    kv = (kv_0, kv_1, kv_2)
    steps = queries.shape[0]
    ahead = products(kv, queries[0], d_out[0])
    for step in range(steps):
        score, d_prob = ahead
        if step < steps - 1:
            ahead = products(kv, queries[step + 1], d_out[step + 1])
        top = largest(score, live)
        expo = exponentials(score, top, live)
        expo_out[step] = expo
        d_prob_out[step] = d_prob
        stats[step, 0:1] = top
        stats[step, 1:2] = jnp.sum(expo, axis=0, keepdims=True)
        stats[step, 2:3] = jnp.sum(expo * d_prob, axis=0, keepdims=True)


def main_kernel(
    live_tiles, expo_1, d_prob_1, stats, kv_3, queries, d_out, d_score, partial, acc_k, acc_v
):
    f32, bf16 = jnp.float32, jnp.bfloat16
    live = [place < live_tiles[0:1, 0:1] for place in places()[3:]]
    kv = (kv_3,)
    steps, before = queries.shape[0], expo_1.shape[1]
    ahead = products(kv, queries[0], d_out[0])
    for step in range(steps):
        q, s = queries[step], d_out[step]
        score, d_prob = ahead
        if step < steps - 1:
            ahead = products(kv, queries[step + 1], d_out[step + 1])
        top_1, sum_1, dot_1 = (stats[step, i : i + 1] for i in range(3))
        top = jnp.maximum(top_1, largest(score, live))
        expo = exponentials(score, top, live)
        weight = jnp.exp2((top_1 - top) * (SCALE * LOG2E))
        inverse = 1.0 / (sum_1 * weight + jnp.sum(expo, axis=0, keepdims=True))
        delta = (dot_1 * weight + jnp.sum(expo * d_prob, axis=0, keepdims=True)) * inverse
        prob_1 = (expo_1[step] * (weight * inverse)).astype(bf16)
        prob_2 = (expo * inverse).astype(bf16)
        d_s_1 = prob_1 * (d_prob_1[step] - delta).astype(bf16)
        d_s_2 = prob_2 * (d_prob - delta).astype(bf16)
        d_score[step, :before] = d_s_1
        d_score[step, before:] = d_s_2
        term_k = jnp.dot(jnp.concatenate([d_s_1, d_s_2], 0), q, preferred_element_type=f32)
        term_v = jnp.dot(jnp.concatenate([prob_1, prob_2], 0), s, preferred_element_type=f32)
        if step == 0:
            acc_k[...] = term_k
            acc_v[...] = term_v
        else:
            acc_k[...] += term_k
            acc_v[...] += term_v
    both = [acc.reshape(PLANE, 8, HD) for acc in (acc_k[...], acc_v[...])]
    both = jnp.concatenate(both, 1).astype(bf16)
    run = PLANE // BLOCKS
    for b, place in enumerate(places()):
        for i in range(run):
            at = lax.bitwise_xor(place, FIRST_ZH) * run + (i ^ FIRST_IN)
            partial[pl.ds(at, 1)] = both[b * run + i : b * run + i + 1]


def query_kernel(gate, kv_0, kv_1, kv_2, kv_3, d_score, d_queries):
    factor = jnp.tanh(gate[...]) * SCALE
    keys_t = stacked((kv_0, kv_1, kv_2, kv_3), 0).T
    rows = d_queries.shape[0]
    for step in range(d_score.shape[0]):
        d_q = jnp.dot(keys_t, d_score[step], preferred_element_type=jnp.float32)
        d_q = (d_q * factor).T.astype(jnp.bfloat16)
        for i in range(HEADS_STEP):
            cols = pl.ds((step * HEADS_STEP + i) * HD, HD)
            d_queries[:, cols] = d_q[i * rows : (i + 1) * rows]


def sum_kernel(gate, pieces, d_keys, d_values):
    factor = jnp.tanh(gate[...])
    heads = PLANE // BLOCKS // 2
    for head in range(heads):
        total = None
        for zh in range(BLOCKS):
            for c in range(2):
                piece = pieces[(zh * heads + (head ^ FIRST_IN // 2)) * 2 + c].astype(jnp.float32)
                total = piece if total is None else total + piece
        cols = pl.ds(head * HD, HD)
        d_keys[:, cols] = total[:8] * (factor * SCALE)
        d_values[:, cols] = total[8:] * factor


def in_vmem(array):
    return pltpu.with_memory_space_constraint(array, pltpu.VMEM)


def in_hbm(array):
    return pltpu.with_memory_space_constraint(array, pltpu.HBM)


def swap(value, step):
    pairs = []
    for c in range(2):
        for group in GROUPS:
            pairs += [(2 * group[i] + c, 2 * group[i ^ step[c]] + c) for i in range(BLOCKS)]
    return in_vmem(lax.ppermute(value, ("zh", "zl", "c"), pairs))


def local(queries, keys, values, d_out, gate, tiles, text_len):
    f32, bf16 = jnp.float32, jnp.bfloat16
    gate = gate.reshape(1, 1)
    block, width = keys.shape
    rows, width_q = queries.shape
    steps = width_q // HD // HEADS_STEP
    image = BLOCKS * block
    own, first, second = pl.pallas_call(
        pick_kernel,
        out_shape=(pltpu.VMEM((2, block, HD), bf16),) * 3,
        in_specs=[HBM, HBM],
        out_specs=(VMEM,) * 3,
        scratch_shapes=[pltpu.VMEM((2, block, width), bf16), pltpu.SemaphoreType.DMA((2,))],
        name="pick",
    )(in_hbm(keys), in_hbm(values))
    kv_0, kv_1, kv_2 = in_vmem(own), swap(first, (2, 3)), swap(second, (1, 1))
    kv_3 = in_vmem(lax.ppermute(kv_1, "c", [(0, 1), (1, 0)]))
    by_step = (steps, rows * HEADS_STEP, HD)
    q, d_live, live_tiles = pl.pallas_call(
        prepare_kernel,
        out_shape=(
            pltpu.VMEM(by_step, bf16),
            pltpu.VMEM(by_step, bf16),
            pltpu.VMEM((8, HD), jnp.int32),
        ),
        in_specs=[HBM] * 4,
        out_specs=(VMEM,) * 3,
        scratch_shapes=[
            pltpu.SMEM(tiles.shape, jnp.int32),
            pltpu.SMEM(text_len.shape, jnp.int32),
            pltpu.VMEM(queries.shape, bf16),
            pltpu.VMEM(queries.shape, bf16),
            pltpu.SemaphoreType.DMA((4,)),
        ],
        compiler_params=pltpu.CompilerParams(vmem_limit_bytes=16 * 2**20),
        cost_estimate=pl.CostEstimate(
            flops=4 * rows * width_q, bytes_accessed=8 * rows * width_q, transcendentals=0
        ),
        name="prepare",
    )(*(in_hbm(array) for array in (tiles, text_len, queries, d_out)))
    q, d_live, live_tiles = in_vmem(q), in_vmem(d_live), in_vmem(live_tiles)
    by_part = (steps, image - block, rows * HEADS_STEP)
    expo, d_prob, stats = pl.pallas_call(
        first_kernel,
        out_shape=(
            pltpu.VMEM(by_part, f32),
            pltpu.VMEM(by_part, f32),
            pltpu.VMEM((steps, 8, rows * HEADS_STEP), f32),
        ),
        in_specs=[VMEM] * 6,
        out_specs=(VMEM,) * 3,
        compiler_params=pltpu.CompilerParams(vmem_limit_bytes=24 * 2**20),
        cost_estimate=pl.CostEstimate(
            flops=40 * rows * width_q * image, bytes_accessed=rows * width_q, transcendentals=0
        ),
        name="three_blocks",
    )(live_tiles, kv_0, kv_1, kv_2, q, d_live)
    d_score, partial = pl.pallas_call(
        main_kernel,
        out_shape=(
            pltpu.VMEM((steps, image, rows * HEADS_STEP), bf16),
            pltpu.VMEM((PLANE, 16, HD), bf16),
        ),
        in_specs=[VMEM] * 7,
        out_specs=(VMEM, VMEM),
        scratch_shapes=[pltpu.VMEM((image, HD), f32), pltpu.VMEM((image, HD), f32)],
        compiler_params=pltpu.CompilerParams(vmem_limit_bytes=36 * 2**20),
        name="gradients",
    )(live_tiles, in_vmem(expo), in_vmem(d_prob), in_vmem(stats), kv_3, q, d_live)
    run = PLANE // BLOCKS
    members = [(zh ^ FIRST_ZH) * run + (i ^ FIRST_IN) for zh in range(BLOCKS) for i in range(run)]
    pieces = lax.all_to_all(partial, ("zh", "x", "zl", "c"), 0, 0, axis_index_groups=[members])
    d_queries = pl.pallas_call(
        query_kernel,
        out_shape=jax.ShapeDtypeStruct(queries.shape, bf16),
        in_specs=[VMEM] * 6,
        out_specs=VMEM,
        compiler_params=pltpu.CompilerParams(vmem_limit_bytes=16 * 2**20),
        cost_estimate=pl.CostEstimate(
            flops=2 * rows * width_q * image, bytes_accessed=4 * rows * width_q, transcendentals=0
        ),
        name="query_gradient",
    )(gate, kv_0, kv_1, kv_2, kv_3, in_vmem(d_score))
    d_keys, d_values = pl.pallas_call(
        sum_kernel,
        out_shape=(jax.ShapeDtypeStruct((8, width), f32),) * 2,
        in_specs=[VMEM, VMEM],
        out_specs=(VMEM, VMEM),
        name="add_up",
    )(gate, in_vmem(pieces))
    return d_queries, d_keys, d_values


def solution(mesh):
    mesh = Mesh(mesh.devices.reshape(SIZES), AXES)
    section, tensor = ("y", "zh"), ("x", "zl", "c")
    in_specs = (
        P(section, tensor),
        P(section, None),
        P(section, None),
        P(section, tensor),
        P(),
        P(),
        P(),
    )
    out_specs = (P(section, tensor), P(AXES, None), P(AXES, None))
    return jax.shard_map(local, mesh=mesh, in_specs=in_specs, out_specs=out_specs, check_vma=False)
```

```python
import jax
import jax.numpy as jnp
from jax import lax
from jax.experimental import pallas as pl
from jax.experimental.pallas import tpu as pltpu
from jax.sharding import Mesh, PartitionSpec as P

HD = 128
TILE = 128
SCALE = HD**-0.5
LOG2E = 1.4426950408889634
AXES = ("y", "zh", "x", "zl", "c")
SIZES = (8, 4, 4, 2, 2)
BLOCKS = 4
HEADS_X = 2
HEADS_STEP = 2
CHIPS = 32
GROUPS = ((1, 2, 4, 7), (0, 3, 5, 6))
FIRST_ZH, FIRST_IN = 2, 5
NT = (((1,), (1,)), ((), ()))
VMEM = pl.BlockSpec(memory_space=pltpu.VMEM)
HBM = pl.BlockSpec(memory_space=pltpu.HBM)


def partner(zh, c):
    return lax.bitwise_xor(zh, 2 + c)


def end_of(zh):
    return jnp.where((zh == 0) | (zh == BLOCKS - 1), 1, 0)


def pick_kernel(keys, values, own, first, second, blocks, sems):
    x, zh, zl, c = (lax.axis_index(axis) for axis in ("x", "zh", "zl", "c"))
    copies = [
        pltpu.make_async_copy(source, blocks.at[k], sems.at[k])
        for k, source in enumerate((keys, values))
    ]
    for copy in copies:
        copy.start()
    flip = lax.rem(end_of(zh) + zl, 2)
    for k in range(2):
        copies[k].wait()
        for section, out in ((zh, own), (partner(zh, c), first), (lax.bitwise_xor(zh, 1), second)):
            head = x * HEADS_X + lax.rem(end_of(section) + flip, 2)
            out[k] = blocks[k, :, pl.ds(pl.multiple_of(head * HD, HD), HD)]


def prepare_kernel(
    tiles, text_len, queries, d_out, q_out, d_live, live_tiles, s_tiles, s_text, q, d, sems
):
    pairs = ((d_out, d), (queries, q), (text_len, s_text), (tiles, s_tiles))
    copies = [pltpu.make_async_copy(*pair, sems.at[i]) for i, pair in enumerate(pairs)]
    for copy in copies:
        copy.start()
    for copy in copies:
        copy.wait()
    y, zh = lax.axis_index("y"), lax.axis_index("zh")
    live_tiles[...] = jnp.full(live_tiles.shape, s_tiles[y], jnp.int32)
    rows, heads = queries.shape[0], queries.shape[1] // HD
    live = lax.broadcasted_iota(jnp.int32, (rows, HD), 0) + zh * rows < s_text[y]
    for h in range(heads):
        cols = pl.ds(h * HD, HD)
        step, place = h // HEADS_STEP, pl.ds(h % HEADS_STEP * rows, rows)
        q_out[step, place] = q[:, cols]
        d_live[step, place] = jnp.where(live, d[:, cols].astype(jnp.float32), 0.0).astype(jnp.bfloat16)


def stacked(parts, k):
    return jnp.concatenate([part[k] for part in parts], 0)


def products(parts, q, s):
    score = lax.dot_general(stacked(parts, 0), q, NT, preferred_element_type=jnp.float32)
    d_prob = lax.dot_general(stacked(parts, 1), s, NT, preferred_element_type=jnp.float32)
    return score, d_prob


def largest(score, live):
    top = -3e38
    for b in range(len(live)):
        part = jnp.max(score[b * TILE : (b + 1) * TILE], axis=0, keepdims=True)
        top = jnp.maximum(top, jnp.where(live[b], part, -3e38))
    return top


def exponentials(score, top, live):
    parts = []
    for b in range(len(live)):
        shift = jnp.where(live[b], top, 1e30)
        parts.append(jnp.exp2((score[b * TILE : (b + 1) * TILE] - shift) * (SCALE * LOG2E)))
    return jnp.concatenate(parts, 0)


def places():
    zh, c = lax.axis_index("zh"), lax.axis_index("c")
    return zh, partner(zh, c), lax.bitwise_xor(zh, 1), partner(zh, 1 - c)


def first_kernel(live_tiles, kv_0, kv_1, kv_2, queries, d_out, expo_out, d_prob_out, stats):
    live = [place < live_tiles[0:1, 0:1] for place in places()[:3]]
    kv = (kv_0, kv_1, kv_2)
    steps = queries.shape[0]
    ahead = products(kv, queries[0], d_out[0])
    for step in range(steps):
        score, d_prob = ahead
        if step < steps - 1:
            ahead = products(kv, queries[step + 1], d_out[step + 1])
        top = largest(score, live)
        expo = exponentials(score, top, live)
        expo_out[step] = expo
        d_prob_out[step] = d_prob
        stats[step, 0:1] = top
        stats[step, 1:2] = jnp.sum(expo, axis=0, keepdims=True)
        stats[step, 2:3] = jnp.sum(expo * d_prob, axis=0, keepdims=True)


def main_kernel(
    live_tiles, expo_1, d_prob_1, stats, kv_3, queries, d_out, d_score, keep, send, acc_k, acc_v
):
    f32, bf16 = jnp.float32, jnp.bfloat16
    live = [place < live_tiles[0:1, 0:1] for place in places()[3:]]
    kv = (kv_3,)
    steps, before = queries.shape[0], expo_1.shape[1]
    ahead = products(kv, queries[0], d_out[0])
    for step in range(steps):
        q, s = queries[step], d_out[step]
        score, d_prob = ahead
        if step < steps - 1:
            ahead = products(kv, queries[step + 1], d_out[step + 1])
        top_1, sum_1, dot_1 = (stats[step, i : i + 1] for i in range(3))
        top = jnp.maximum(top_1, largest(score, live))
        expo = exponentials(score, top, live)
        weight = jnp.exp2((top_1 - top) * (SCALE * LOG2E))
        inverse = 1.0 / (sum_1 * weight + jnp.sum(expo, axis=0, keepdims=True))
        delta = (dot_1 * weight + jnp.sum(expo * d_prob, axis=0, keepdims=True)) * inverse
        prob_1 = (expo_1[step] * (weight * inverse)).astype(bf16)
        prob_2 = (expo * inverse).astype(bf16)
        d_s_1 = prob_1 * (d_prob_1[step] - delta).astype(bf16)
        d_s_2 = prob_2 * (d_prob - delta).astype(bf16)
        d_score[step, :before] = d_s_1
        d_score[step, before:] = d_s_2
        term_k = jnp.dot(jnp.concatenate([d_s_1, d_s_2], 0), q, preferred_element_type=f32)
        term_v = jnp.dot(jnp.concatenate([prob_1, prob_2], 0), s, preferred_element_type=f32)
        if step == 0:
            acc_k[...] = term_k
            acc_v[...] = term_v
        else:
            acc_k[...] += term_k
            acc_v[...] += term_v
    both = [acc.reshape(CHIPS, 2, 8, HD) for acc in (acc_k[...], acc_v[...])]
    both = jnp.concatenate(both, 2)
    even = lax.axis_index("c") == 0
    mine, other = jnp.where(even, both[:, 0], both[:, 1]), jnp.where(even, both[:, 1], both[:, 0])
    other = other.astype(bf16)
    run = CHIPS // BLOCKS
    for b, place in enumerate(places()):
        for i in range(run):
            at = pl.ds(lax.bitwise_xor(place, FIRST_ZH) * run + (i ^ FIRST_IN), 1)
            keep[at] = mine[b * run + i : b * run + i + 1]
            send[at] = other[b * run + i : b * run + i + 1]


def chip_kernel(keep, other, partial):
    partial[...] = (keep[...] + other[...].astype(jnp.float32)).astype(jnp.bfloat16)


def query_kernel(gate, kv_0, kv_1, kv_2, kv_3, d_score, d_queries):
    factor = jnp.tanh(gate[...]) * SCALE
    keys_t = stacked((kv_0, kv_1, kv_2, kv_3), 0).T
    rows = d_queries.shape[0]
    for step in range(d_score.shape[0]):
        d_q = jnp.dot(keys_t, d_score[step], preferred_element_type=jnp.float32)
        d_q = (d_q * factor).T.astype(jnp.bfloat16)
        for i in range(HEADS_STEP):
            cols = pl.ds((step * HEADS_STEP + i) * HD, HD)
            d_queries[:, cols] = d_q[i * rows : (i + 1) * rows]


def sum_kernel(gate, pieces, d_keys, d_values):
    factor = jnp.tanh(gate[...])
    heads = CHIPS // BLOCKS
    for head in range(heads):
        total = None
        for zh in range(BLOCKS):
            piece = pieces[zh * heads + (head ^ FIRST_IN)].astype(jnp.float32)
            total = piece if total is None else total + piece
        cols = pl.ds(head * HD, HD)
        d_keys[:, cols] = total[:8] * (factor * SCALE)
        d_values[:, cols] = total[8:] * factor


def in_vmem(array):
    return pltpu.with_memory_space_constraint(array, pltpu.VMEM)


def in_hbm(array):
    return pltpu.with_memory_space_constraint(array, pltpu.HBM)


def swap(value, step):
    pairs = []
    for c in range(2):
        for group in GROUPS:
            pairs += [(2 * group[i] + c, 2 * group[i ^ step[c]] + c) for i in range(BLOCKS)]
    return in_vmem(lax.ppermute(value, ("zh", "zl", "c"), pairs))


def local(queries, keys, values, d_out, gate, tiles, text_len):
    f32, bf16 = jnp.float32, jnp.bfloat16
    gate = gate.reshape(1, 1)
    block, width = keys.shape
    rows, width_q = queries.shape
    steps = width_q // HD // HEADS_STEP
    image = BLOCKS * block
    own, first, second = pl.pallas_call(
        pick_kernel,
        out_shape=(pltpu.VMEM((2, block, HD), bf16),) * 3,
        in_specs=[HBM, HBM],
        out_specs=(VMEM,) * 3,
        scratch_shapes=[pltpu.VMEM((2, block, width), bf16), pltpu.SemaphoreType.DMA((2,))],
        name="pick",
    )(in_hbm(keys), in_hbm(values))
    kv_0, kv_1, kv_2 = in_vmem(own), swap(first, (2, 3)), swap(second, (1, 1))
    kv_3 = in_vmem(lax.ppermute(kv_1, "c", [(0, 1), (1, 0)]))
    by_step = (steps, rows * HEADS_STEP, HD)
    q, d_live, live_tiles = pl.pallas_call(
        prepare_kernel,
        out_shape=(
            pltpu.VMEM(by_step, bf16),
            pltpu.VMEM(by_step, bf16),
            pltpu.VMEM((8, HD), jnp.int32),
        ),
        in_specs=[HBM] * 4,
        out_specs=(VMEM,) * 3,
        scratch_shapes=[
            pltpu.SMEM(tiles.shape, jnp.int32),
            pltpu.SMEM(text_len.shape, jnp.int32),
            pltpu.VMEM(queries.shape, bf16),
            pltpu.VMEM(queries.shape, bf16),
            pltpu.SemaphoreType.DMA((4,)),
        ],
        compiler_params=pltpu.CompilerParams(vmem_limit_bytes=16 * 2**20),
        cost_estimate=pl.CostEstimate(
            flops=4 * rows * width_q, bytes_accessed=8 * rows * width_q, transcendentals=0
        ),
        name="prepare",
    )(*(in_hbm(array) for array in (tiles, text_len, queries, d_out)))
    q, d_live, live_tiles = in_vmem(q), in_vmem(d_live), in_vmem(live_tiles)
    by_part = (steps, image - block, rows * HEADS_STEP)
    expo, d_prob, stats = pl.pallas_call(
        first_kernel,
        out_shape=(
            pltpu.VMEM(by_part, f32),
            pltpu.VMEM(by_part, f32),
            pltpu.VMEM((steps, 8, rows * HEADS_STEP), f32),
        ),
        in_specs=[VMEM] * 6,
        out_specs=(VMEM,) * 3,
        compiler_params=pltpu.CompilerParams(vmem_limit_bytes=24 * 2**20),
        cost_estimate=pl.CostEstimate(
            flops=40 * rows * width_q * image, bytes_accessed=rows * width_q, transcendentals=0
        ),
        name="three_blocks",
    )(live_tiles, kv_0, kv_1, kv_2, q, d_live)
    d_score, keep, send = pl.pallas_call(
        main_kernel,
        out_shape=(
            pltpu.VMEM((steps, image, rows * HEADS_STEP), bf16),
            pltpu.VMEM((CHIPS, 16, HD), f32),
            pltpu.VMEM((CHIPS, 16, HD), bf16),
        ),
        in_specs=[VMEM] * 7,
        out_specs=(VMEM,) * 3,
        scratch_shapes=[pltpu.VMEM((image, HD), f32), pltpu.VMEM((image, HD), f32)],
        compiler_params=pltpu.CompilerParams(vmem_limit_bytes=36 * 2**20),
        name="gradients",
    )(live_tiles, in_vmem(expo), in_vmem(d_prob), in_vmem(stats), kv_3, q, d_live)
    other = lax.ppermute(send, "c", [(0, 1), (1, 0)])
    partial = pl.pallas_call(
        chip_kernel,
        out_shape=jax.ShapeDtypeStruct((CHIPS, 16, HD), bf16),
        in_specs=[VMEM, VMEM],
        out_specs=VMEM,
        name="add_cores",
    )(in_vmem(keep), in_vmem(other))
    run = CHIPS // BLOCKS
    members = [(zh ^ FIRST_ZH) * run + (i ^ FIRST_IN) for zh in range(BLOCKS) for i in range(run)]
    pieces = lax.all_to_all(partial, ("zh", "x", "zl"), 0, 0, axis_index_groups=[members])
    d_queries = pl.pallas_call(
        query_kernel,
        out_shape=jax.ShapeDtypeStruct(queries.shape, bf16),
        in_specs=[VMEM] * 6,
        out_specs=VMEM,
        compiler_params=pltpu.CompilerParams(vmem_limit_bytes=16 * 2**20),
        cost_estimate=pl.CostEstimate(
            flops=2 * rows * width_q * image, bytes_accessed=4 * rows * width_q, transcendentals=0
        ),
        name="query_gradient",
    )(gate, kv_0, kv_1, kv_2, kv_3, in_vmem(d_score))
    d_keys, d_values = pl.pallas_call(
        sum_kernel,
        out_shape=(jax.ShapeDtypeStruct((8, width), f32),) * 2,
        in_specs=[VMEM, VMEM],
        out_specs=(VMEM, VMEM),
        name="add_up",
    )(gate, in_vmem(pieces))
    return d_queries, d_keys, d_values


def solution(mesh):
    mesh = Mesh(mesh.devices.reshape(SIZES), AXES)
    section, tensor = ("y", "zh"), ("x", "zl", "c")
    in_specs = (
        P(section, tensor),
        P(section, None),
        P(section, None),
        P(section, tensor),
        P(),
        P(),
        P(),
    )
    out_specs = (P(section, tensor), P(AXES, None), P(AXES, None))
    return jax.shard_map(local, mesh=mesh, in_specs=in_specs, out_specs=out_specs, check_vma=False)
```

```python
import jax
import jax.numpy as jnp
from jax import lax
from jax.experimental import pallas as pl
from jax.experimental.pallas import tpu as pltpu
from jax.sharding import Mesh, PartitionSpec as P

HD = 128
TILE = 128
SCALE = HD**-0.5
LOG2E = 1.4426950408889634
AXES = ("y", "zh", "x", "zl", "c")
SIZES = (8, 4, 4, 2, 2)
BLOCKS = 4
HEADS_X = 2
HEADS_STEP = 2
CHIPS = 32
GROUPS = ((1, 2, 4, 7), (0, 3, 5, 6))
FIRST_ZH, FIRST_IN = 2, 5
NT = (((1,), (1,)), ((), ()))
VMEM = pl.BlockSpec(memory_space=pltpu.VMEM)
HBM = pl.BlockSpec(memory_space=pltpu.HBM)


def partner(zh, c):
    return lax.bitwise_xor(zh, 2 + c)


def end_of(zh):
    return jnp.where((zh == 0) | (zh == BLOCKS - 1), 1, 0)


def pick_kernel(keys, values, own, first, second, blocks, sems):
    x, zh, zl, c = (lax.axis_index(axis) for axis in ("x", "zh", "zl", "c"))
    copies = [
        pltpu.make_async_copy(source, blocks.at[k], sems.at[k])
        for k, source in enumerate((keys, values))
    ]
    for copy in copies:
        copy.start()
    flip = lax.rem(end_of(zh) + zl, 2)
    for k in range(2):
        copies[k].wait()
        for section, out in ((zh, own), (partner(zh, c), first), (lax.bitwise_xor(zh, 1), second)):
            head = x * HEADS_X + lax.rem(end_of(section) + flip, 2)
            out[k] = blocks[k, :, pl.ds(pl.multiple_of(head * HD, HD), HD)]


def prepare_kernel(
    tiles, text_len, queries, d_out, gate, q_out, d_live, live_tiles, factor, s_tiles, s_text, q, d, sems
):
    pairs = ((d_out, d), (queries, q), (text_len, s_text), (tiles, s_tiles))
    copies = [pltpu.make_async_copy(*pair, sems.at[i]) for i, pair in enumerate(pairs)]
    for copy in copies:
        copy.start()
    for copy in copies:
        copy.wait()
    y, zh = lax.axis_index("y"), lax.axis_index("zh")
    live_tiles[...] = jnp.full(live_tiles.shape, s_tiles[y], jnp.int32)
    factor[...] = jnp.broadcast_to(jnp.tanh(gate[...]), factor.shape)
    rows, heads = queries.shape[0], queries.shape[1] // HD
    live = lax.broadcasted_iota(jnp.int32, (rows, HD), 0) + zh * rows < s_text[y]
    for h in range(heads):
        cols = pl.ds(h * HD, HD)
        step, place = h // HEADS_STEP, pl.ds(h % HEADS_STEP * rows, rows)
        q_out[step, place] = q[:, cols]
        d_live[step, place] = jnp.where(live, d[:, cols].astype(jnp.float32), 0.0).astype(jnp.bfloat16)


def stacked(parts, k):
    return jnp.concatenate([part[k] for part in parts], 0)


def products(parts, q, s):
    score = lax.dot_general(stacked(parts, 0), q, NT, preferred_element_type=jnp.float32)
    d_prob = lax.dot_general(stacked(parts, 1), s, NT, preferred_element_type=jnp.float32)
    return score, d_prob


def largest(score, live):
    top = -3e38
    for b in range(len(live)):
        part = jnp.max(score[b * TILE : (b + 1) * TILE], axis=0, keepdims=True)
        top = jnp.maximum(top, jnp.where(live[b], part, -3e38))
    return top


def exponentials(score, top, live):
    parts = []
    for b in range(len(live)):
        shift = jnp.where(live[b], top, 1e30)
        parts.append(jnp.exp2((score[b * TILE : (b + 1) * TILE] - shift) * (SCALE * LOG2E)))
    return jnp.concatenate(parts, 0)


def places():
    zh, c = lax.axis_index("zh"), lax.axis_index("c")
    return zh, partner(zh, c), lax.bitwise_xor(zh, 1), partner(zh, 1 - c)


def first_kernel(live_tiles, kv_0, kv_1, kv_2, queries, d_out, expo_out, d_prob_out, stats):
    live = [place < live_tiles[0:1, 0:1] for place in places()[:3]]
    kv = (kv_0, kv_1, kv_2)
    steps = queries.shape[0]
    ahead = products(kv, queries[0], d_out[0])
    for step in range(steps):
        score, d_prob = ahead
        if step < steps - 1:
            ahead = products(kv, queries[step + 1], d_out[step + 1])
        top = largest(score, live)
        expo = exponentials(score, top, live)
        expo_out[step] = expo
        d_prob_out[step] = d_prob
        stats[step, 0:1] = top
        stats[step, 1:2] = jnp.sum(expo, axis=0, keepdims=True)
        stats[step, 2:3] = jnp.sum(expo * d_prob, axis=0, keepdims=True)


def main_kernel(
    live_tiles, expo_1, d_prob_1, stats, kv_3, queries, d_out, d_score, keep, send, acc_k, acc_v
):
    f32, bf16 = jnp.float32, jnp.bfloat16
    live = [place < live_tiles[0:1, 0:1] for place in places()[3:]]
    kv = (kv_3,)
    steps, before = queries.shape[0], expo_1.shape[1]
    ahead = products(kv, queries[0], d_out[0])
    for step in range(steps):
        q, s = queries[step], d_out[step]
        score, d_prob = ahead
        if step < steps - 1:
            ahead = products(kv, queries[step + 1], d_out[step + 1])
        top_1, sum_1, dot_1 = (stats[step, i : i + 1] for i in range(3))
        top = jnp.maximum(top_1, largest(score, live))
        expo = exponentials(score, top, live)
        weight = jnp.exp2((top_1 - top) * (SCALE * LOG2E))
        inverse = 1.0 / (sum_1 * weight + jnp.sum(expo, axis=0, keepdims=True))
        delta = (dot_1 * weight + jnp.sum(expo * d_prob, axis=0, keepdims=True)) * inverse
        prob_1 = (expo_1[step] * (weight * inverse)).astype(bf16)
        prob_2 = (expo * inverse).astype(bf16)
        d_s_1 = prob_1 * (d_prob_1[step] - delta).astype(bf16)
        d_s_2 = prob_2 * (d_prob - delta).astype(bf16)
        d_score[step, :before] = d_s_1
        d_score[step, before:] = d_s_2
        term_k = jnp.dot(jnp.concatenate([d_s_1, d_s_2], 0), q, preferred_element_type=f32)
        term_v = jnp.dot(jnp.concatenate([prob_1, prob_2], 0), s, preferred_element_type=f32)
        if step == 0:
            acc_k[...] = term_k
            acc_v[...] = term_v
        else:
            acc_k[...] += term_k
            acc_v[...] += term_v
    both = [acc.reshape(CHIPS, 2, 8, HD) for acc in (acc_k[...], acc_v[...])]
    both = jnp.concatenate(both, 2)
    even = lax.axis_index("c") == 0
    mine, other = jnp.where(even, both[:, 0], both[:, 1]), jnp.where(even, both[:, 1], both[:, 0])
    other = other.astype(bf16)
    run = CHIPS // BLOCKS
    for b, place in enumerate(places()):
        for i in range(run):
            at = pl.ds(lax.bitwise_xor(place, FIRST_ZH) * run + (i ^ FIRST_IN), 1)
            keep[at] = mine[b * run + i : b * run + i + 1]
            send[at] = other[b * run + i : b * run + i + 1]


def chip_kernel(keep, other, _, partial):
    partial[...] = (keep[...] + other[...].astype(jnp.float32)).astype(jnp.bfloat16)


def query_kernel(gate_factor, kv_0, kv_1, kv_2, kv_3, d_score, d_queries):
    factor = gate_factor[0:1, 0:1] * SCALE
    keys_t = stacked((kv_0, kv_1, kv_2, kv_3), 0).T
    rows = d_queries.shape[0]
    for step in range(d_score.shape[0]):
        d_q = jnp.dot(keys_t, d_score[step], preferred_element_type=jnp.float32)
        d_q = (d_q * factor).T.astype(jnp.bfloat16)
        for i in range(HEADS_STEP):
            cols = pl.ds((step * HEADS_STEP + i) * HD, HD)
            d_queries[:, cols] = d_q[i * rows : (i + 1) * rows]


def sum_kernel(gate_factor, pieces, d_keys, d_values):
    factor = gate_factor[0:1]
    heads = CHIPS // BLOCKS
    for head in range(heads):
        total = None
        for zh in range(BLOCKS):
            piece = pieces[zh * heads + (head ^ FIRST_IN)].astype(jnp.float32)
            total = piece if total is None else total + piece
        cols = pl.ds(head * HD, HD)
        d_keys[:, cols] = total[:8] * (factor * SCALE)
        d_values[:, cols] = total[8:] * factor


def in_vmem(array):
    return pltpu.with_memory_space_constraint(array, pltpu.VMEM)


def in_hbm(array):
    return pltpu.with_memory_space_constraint(array, pltpu.HBM)


def swap(value, step):
    pairs = []
    for c in range(2):
        for group in GROUPS:
            pairs += [(2 * group[i] + c, 2 * group[i ^ step[c]] + c) for i in range(BLOCKS)]
    return in_vmem(lax.ppermute(value, ("zh", "zl", "c"), pairs))


def local(queries, keys, values, d_out, gate, tiles, text_len):
    f32, bf16 = jnp.float32, jnp.bfloat16
    gate = gate.reshape(1, 1)
    block, width = keys.shape
    rows, width_q = queries.shape
    steps = width_q // HD // HEADS_STEP
    image = BLOCKS * block
    own, first, second = pl.pallas_call(
        pick_kernel,
        out_shape=(pltpu.VMEM((2, block, HD), bf16),) * 3,
        in_specs=[HBM, HBM],
        out_specs=(VMEM,) * 3,
        scratch_shapes=[pltpu.VMEM((2, block, width), bf16), pltpu.SemaphoreType.DMA((2,))],
        name="pick",
    )(in_hbm(keys), in_hbm(values))
    kv_0, kv_1, kv_2 = in_vmem(own), swap(first, (2, 3)), swap(second, (1, 1))
    kv_3 = in_vmem(lax.ppermute(kv_1, "c", [(0, 1), (1, 0)]))
    by_step = (steps, rows * HEADS_STEP, HD)
    q, d_live, live_tiles, factor = pl.pallas_call(
        prepare_kernel,
        out_shape=(
            pltpu.VMEM(by_step, bf16),
            pltpu.VMEM(by_step, bf16),
            pltpu.VMEM((8, HD), jnp.int32),
            pltpu.VMEM((8, HD), f32),
        ),
        in_specs=[HBM] * 4 + [VMEM],
        out_specs=(VMEM,) * 4,
        scratch_shapes=[
            pltpu.SMEM(tiles.shape, jnp.int32),
            pltpu.SMEM(text_len.shape, jnp.int32),
            pltpu.VMEM(queries.shape, bf16),
            pltpu.VMEM(queries.shape, bf16),
            pltpu.SemaphoreType.DMA((4,)),
        ],
        compiler_params=pltpu.CompilerParams(vmem_limit_bytes=16 * 2**20),
        cost_estimate=pl.CostEstimate(
            flops=4 * rows * width_q, bytes_accessed=8 * rows * width_q, transcendentals=0
        ),
        name="prepare",
    )(*(in_hbm(array) for array in (tiles, text_len, queries, d_out)), gate)
    q, d_live, live_tiles, factor = (in_vmem(array) for array in (q, d_live, live_tiles, factor))
    by_part = (steps, image - block, rows * HEADS_STEP)
    expo, d_prob, stats = pl.pallas_call(
        first_kernel,
        out_shape=(
            pltpu.VMEM(by_part, f32),
            pltpu.VMEM(by_part, f32),
            pltpu.VMEM((steps, 8, rows * HEADS_STEP), f32),
        ),
        in_specs=[VMEM] * 6,
        out_specs=(VMEM,) * 3,
        compiler_params=pltpu.CompilerParams(vmem_limit_bytes=24 * 2**20),
        cost_estimate=pl.CostEstimate(
            flops=40 * rows * width_q * image, bytes_accessed=rows * width_q, transcendentals=0
        ),
        name="three_blocks",
    )(live_tiles, kv_0, kv_1, kv_2, q, d_live)
    d_score, keep, send = pl.pallas_call(
        main_kernel,
        out_shape=(
            pltpu.VMEM((steps, image, rows * HEADS_STEP), bf16),
            pltpu.VMEM((CHIPS, 16, HD), f32),
            pltpu.VMEM((CHIPS, 16, HD), bf16),
        ),
        in_specs=[VMEM] * 7,
        out_specs=(VMEM,) * 3,
        scratch_shapes=[pltpu.VMEM((image, HD), f32), pltpu.VMEM((image, HD), f32)],
        compiler_params=pltpu.CompilerParams(vmem_limit_bytes=36 * 2**20),
        name="gradients",
    )(live_tiles, in_vmem(expo), in_vmem(d_prob), in_vmem(stats), kv_3, q, d_live)
    other = lax.ppermute(send, "c", [(0, 1), (1, 0)])
    d_queries = pl.pallas_call(
        query_kernel,
        out_shape=jax.ShapeDtypeStruct(queries.shape, bf16),
        in_specs=[VMEM] * 6,
        out_specs=VMEM,
        compiler_params=pltpu.CompilerParams(vmem_limit_bytes=16 * 2**20),
        cost_estimate=pl.CostEstimate(
            flops=2 * rows * width_q * image, bytes_accessed=4 * rows * width_q, transcendentals=0
        ),
        name="query_gradient",
    )(factor, kv_0, kv_1, kv_2, kv_3, in_vmem(d_score))
    partial = pl.pallas_call(
        chip_kernel,
        out_shape=pltpu.VMEM((CHIPS, 16, HD), bf16),
        in_specs=[VMEM, VMEM, HBM],
        out_specs=VMEM,
        name="add_cores",
    )(in_vmem(keep), in_vmem(other), in_hbm(d_queries))
    run = CHIPS // BLOCKS
    members = [(zh ^ FIRST_ZH) * run + (i ^ FIRST_IN) for zh in range(BLOCKS) for i in range(run)]
    pieces = lax.all_to_all(partial, ("zh", "x", "zl"), 0, 0, axis_index_groups=[members])
    d_keys, d_values = pl.pallas_call(
        sum_kernel,
        out_shape=(jax.ShapeDtypeStruct((8, width), f32),) * 2,
        in_specs=[VMEM, VMEM],
        out_specs=(VMEM, VMEM),
        name="add_up",
    )(factor, in_vmem(pieces))
    return d_queries, d_keys, d_values


def solution(mesh):
    mesh = Mesh(mesh.devices.reshape(SIZES), AXES)
    section, tensor = ("y", "zh"), ("x", "zl", "c")
    in_specs = (
        P(section, tensor),
        P(section, None),
        P(section, None),
        P(section, tensor),
        P(),
        P(),
        P(),
    )
    out_specs = (P(section, tensor), P(AXES, None), P(AXES, None))
    return jax.shard_map(local, mesh=mesh, in_specs=in_specs, out_specs=out_specs, check_vma=False)
```

```python
import jax
import jax.numpy as jnp
from jax import lax
from jax.experimental import pallas as pl
from jax.experimental.pallas import tpu as pltpu
from jax.sharding import Mesh, PartitionSpec as P

HD = 128
TILE = 128
SCALE = HD**-0.5
LOG2E = 1.4426950408889634
AXES = ("y", "zh", "x", "zl", "c")
SIZES = (8, 4, 4, 2, 2)
BLOCKS = 4
HEADS_X = 2
HEADS_STEP = 2
CHIPS = 32
GROUPS = ((1, 2, 4, 7), (0, 3, 5, 6))
FIRST_ZH, FIRST_IN = 2, 5
NT = (((1,), (1,)), ((), ()))
VMEM = pl.BlockSpec(memory_space=pltpu.VMEM)
HBM = pl.BlockSpec(memory_space=pltpu.HBM)


def partner(zh, c):
    return lax.bitwise_xor(zh, 3 - c)


def end_of(zh):
    return jnp.where((zh == 0) | (zh == BLOCKS - 1), 1, 0)


def pick_kernel(keys, values, own, first, second, blocks, sems):
    x, zh, zl, c = (lax.axis_index(axis) for axis in ("x", "zh", "zl", "c"))
    copies = [
        pltpu.make_async_copy(source, blocks.at[k], sems.at[k])
        for k, source in enumerate((keys, values))
    ]
    for copy in copies:
        copy.start()
    flip = lax.rem(end_of(zh) + zl, 2)
    for k in range(2):
        copies[k].wait()
        for section, out in ((zh, own), (partner(zh, c), first), (lax.bitwise_xor(zh, 1), second)):
            head = x * HEADS_X + lax.rem(end_of(section) + flip, 2)
            out[k] = blocks[k, :, pl.ds(pl.multiple_of(head * HD, HD), HD)]


def prepare_kernel(
    tiles, text_len, queries, d_out, gate, q_out, d_live, live_tiles, factor, s_tiles, s_text, q, d, sems
):
    pairs = ((d_out, d), (queries, q), (text_len, s_text), (tiles, s_tiles))
    copies = [pltpu.make_async_copy(*pair, sems.at[i]) for i, pair in enumerate(pairs)]
    for copy in copies:
        copy.start()
    for copy in copies:
        copy.wait()
    y, zh = lax.axis_index("y"), lax.axis_index("zh")
    live_tiles[...] = jnp.full(live_tiles.shape, s_tiles[y], jnp.int32)
    factor[...] = jnp.broadcast_to(jnp.tanh(gate[...]), factor.shape)
    rows, heads = queries.shape[0], queries.shape[1] // HD
    live = lax.broadcasted_iota(jnp.int32, (rows, HD), 0) + zh * rows < s_text[y]
    for h in range(heads):
        cols = pl.ds(h * HD, HD)
        step, place = h // HEADS_STEP, pl.ds(h % HEADS_STEP * rows, rows)
        q_out[step, place] = q[:, cols]
        d_live[step, place] = jnp.where(live, d[:, cols].astype(jnp.float32), 0.0).astype(jnp.bfloat16)


def stacked(parts, k):
    return jnp.concatenate([part[k] for part in parts], 0)


def products(parts, q, s):
    score = lax.dot_general(stacked(parts, 0), q, NT, preferred_element_type=jnp.float32)
    d_prob = lax.dot_general(stacked(parts, 1), s, NT, preferred_element_type=jnp.float32)
    return score, d_prob


def largest(score, live):
    top = -3e38
    for b in range(len(live)):
        part = jnp.max(score[b * TILE : (b + 1) * TILE], axis=0, keepdims=True)
        top = jnp.maximum(top, jnp.where(live[b], part, -3e38))
    return top


def exponentials(score, top, live):
    parts = []
    for b in range(len(live)):
        shift = jnp.where(live[b], top, 1e30)
        parts.append(jnp.exp2((score[b * TILE : (b + 1) * TILE] - shift) * (SCALE * LOG2E)))
    return jnp.concatenate(parts, 0)


def places():
    zh, c = lax.axis_index("zh"), lax.axis_index("c")
    return zh, partner(zh, c), lax.bitwise_xor(zh, 1), partner(zh, 1 - c)


def first_kernel(live_tiles, kv_0, kv_1, kv_2, queries, d_out, expo_out, d_prob_out, stats):
    live = [place < live_tiles[0:1, 0:1] for place in places()[:3]]
    kv = (kv_0, kv_1, kv_2)
    steps = queries.shape[0]
    ahead = products(kv, queries[0], d_out[0])
    for step in range(steps):
        score, d_prob = ahead
        if step < steps - 1:
            ahead = products(kv, queries[step + 1], d_out[step + 1])
        top = largest(score, live)
        expo = exponentials(score, top, live)
        expo_out[step] = expo
        d_prob_out[step] = d_prob
        stats[step, 0:1] = top
        stats[step, 1:2] = jnp.sum(expo, axis=0, keepdims=True)
        stats[step, 2:3] = jnp.sum(expo * d_prob, axis=0, keepdims=True)


def main_kernel(
    live_tiles, expo_1, d_prob_1, stats, kv_3, queries, d_out, d_score, keep, send, acc_k, acc_v
):
    f32, bf16 = jnp.float32, jnp.bfloat16
    live = [place < live_tiles[0:1, 0:1] for place in places()[3:]]
    kv = (kv_3,)
    steps, before = queries.shape[0], expo_1.shape[1]
    ahead = products(kv, queries[0], d_out[0])
    for step in range(steps):
        q, s = queries[step], d_out[step]
        score, d_prob = ahead
        if step < steps - 1:
            ahead = products(kv, queries[step + 1], d_out[step + 1])
        top_1, sum_1, dot_1 = (stats[step, i : i + 1] for i in range(3))
        top = jnp.maximum(top_1, largest(score, live))
        expo = exponentials(score, top, live)
        weight = jnp.exp2((top_1 - top) * (SCALE * LOG2E))
        inverse = 1.0 / (sum_1 * weight + jnp.sum(expo, axis=0, keepdims=True))
        delta = (dot_1 * weight + jnp.sum(expo * d_prob, axis=0, keepdims=True)) * inverse
        prob_1 = (expo_1[step] * (weight * inverse)).astype(bf16)
        prob_2 = (expo * inverse).astype(bf16)
        d_s_1 = prob_1 * (d_prob_1[step] - delta).astype(bf16)
        d_s_2 = prob_2 * (d_prob - delta).astype(bf16)
        d_score[step, :before] = d_s_1
        d_score[step, before:] = d_s_2
        term_k = jnp.dot(jnp.concatenate([d_s_1, d_s_2], 0), q, preferred_element_type=f32)
        term_v = jnp.dot(jnp.concatenate([prob_1, prob_2], 0), s, preferred_element_type=f32)
        if step == 0:
            acc_k[...] = term_k
            acc_v[...] = term_v
        else:
            acc_k[...] += term_k
            acc_v[...] += term_v
    both = [acc.reshape(CHIPS, 2, 8, HD) for acc in (acc_k[...], acc_v[...])]
    both = jnp.concatenate(both, 2)
    even = lax.axis_index("c") == 0
    mine, other = jnp.where(even, both[:, 0], both[:, 1]), jnp.where(even, both[:, 1], both[:, 0])
    other = other.astype(bf16)
    run = CHIPS // BLOCKS
    for b, place in enumerate(places()):
        for i in range(run):
            at = pl.ds(lax.bitwise_xor(place, FIRST_ZH) * run + (i ^ FIRST_IN), 1)
            keep[at] = mine[b * run + i : b * run + i + 1]
            send[at] = other[b * run + i : b * run + i + 1]


def chip_kernel(keep, other, _, partial):
    partial[...] = (keep[...] + other[...].astype(jnp.float32)).astype(jnp.bfloat16)


def query_kernel(gate_factor, kv_0, kv_1, kv_2, kv_3, d_score, d_queries):
    factor = gate_factor[0:1, 0:1] * SCALE
    keys_t = stacked((kv_0, kv_1, kv_2, kv_3), 0).T
    rows = d_queries.shape[0]
    for step in range(d_score.shape[0]):
        d_q = jnp.dot(keys_t, d_score[step], preferred_element_type=jnp.float32)
        d_q = (d_q * factor).T.astype(jnp.bfloat16)
        for i in range(HEADS_STEP):
            cols = pl.ds((step * HEADS_STEP + i) * HD, HD)
            d_queries[:, cols] = d_q[i * rows : (i + 1) * rows]


def sum_kernel(gate_factor, pieces, d_keys, d_values):
    factor = gate_factor[0:1]
    heads = CHIPS // BLOCKS
    for head in range(heads):
        total = None
        for zh in range(BLOCKS):
            piece = pieces[zh * heads + (head ^ FIRST_IN)].astype(jnp.float32)
            total = piece if total is None else total + piece
        cols = pl.ds(head * HD, HD)
        d_keys[:, cols] = total[:8] * (factor * SCALE)
        d_values[:, cols] = total[8:] * factor


def in_vmem(array):
    return pltpu.with_memory_space_constraint(array, pltpu.VMEM)


def in_hbm(array):
    return pltpu.with_memory_space_constraint(array, pltpu.HBM)


def swap(value, step):
    pairs = []
    for c in range(2):
        for group in GROUPS:
            pairs += [(2 * group[i] + c, 2 * group[i ^ step[c]] + c) for i in range(BLOCKS)]
    return in_vmem(lax.ppermute(value, ("zh", "zl", "c"), pairs))


def local(queries, keys, values, d_out, gate, tiles, text_len):
    f32, bf16 = jnp.float32, jnp.bfloat16
    gate = gate.reshape(1, 1)
    block, width = keys.shape
    rows, width_q = queries.shape
    steps = width_q // HD // HEADS_STEP
    image = BLOCKS * block
    own, first, second = pl.pallas_call(
        pick_kernel,
        out_shape=(pltpu.VMEM((2, block, HD), bf16),) * 3,
        in_specs=[HBM, HBM],
        out_specs=(VMEM,) * 3,
        scratch_shapes=[pltpu.VMEM((2, block, width), bf16), pltpu.SemaphoreType.DMA((2,))],
        name="pick",
    )(in_hbm(keys), in_hbm(values))
    kv_0, kv_1, kv_2 = in_vmem(own), swap(first, (3, 2)), swap(second, (1, 1))
    kv_3 = in_vmem(lax.ppermute(kv_1, "c", [(0, 1), (1, 0)]))
    by_step = (steps, rows * HEADS_STEP, HD)
    q, d_live, live_tiles, factor = pl.pallas_call(
        prepare_kernel,
        out_shape=(
            pltpu.VMEM(by_step, bf16),
            pltpu.VMEM(by_step, bf16),
            pltpu.VMEM((8, HD), jnp.int32),
            pltpu.VMEM((8, HD), f32),
        ),
        in_specs=[HBM] * 4 + [VMEM],
        out_specs=(VMEM,) * 4,
        scratch_shapes=[
            pltpu.SMEM(tiles.shape, jnp.int32),
            pltpu.SMEM(text_len.shape, jnp.int32),
            pltpu.VMEM(queries.shape, bf16),
            pltpu.VMEM(queries.shape, bf16),
            pltpu.SemaphoreType.DMA((4,)),
        ],
        compiler_params=pltpu.CompilerParams(vmem_limit_bytes=16 * 2**20),
        cost_estimate=pl.CostEstimate(
            flops=4 * rows * width_q, bytes_accessed=8 * rows * width_q, transcendentals=0
        ),
        name="prepare",
    )(*(in_hbm(array) for array in (tiles, text_len, queries, d_out)), gate)
    q, d_live, live_tiles, factor = (in_vmem(array) for array in (q, d_live, live_tiles, factor))
    by_part = (steps, image - block, rows * HEADS_STEP)
    expo, d_prob, stats = pl.pallas_call(
        first_kernel,
        out_shape=(
            pltpu.VMEM(by_part, f32),
            pltpu.VMEM(by_part, f32),
            pltpu.VMEM((steps, 8, rows * HEADS_STEP), f32),
        ),
        in_specs=[VMEM] * 6,
        out_specs=(VMEM,) * 3,
        compiler_params=pltpu.CompilerParams(vmem_limit_bytes=24 * 2**20),
        cost_estimate=pl.CostEstimate(
            flops=40 * rows * width_q * image, bytes_accessed=rows * width_q, transcendentals=0
        ),
        name="three_blocks",
    )(live_tiles, kv_0, kv_1, kv_2, q, d_live)
    d_score, keep, send = pl.pallas_call(
        main_kernel,
        out_shape=(
            pltpu.VMEM((steps, image, rows * HEADS_STEP), bf16),
            pltpu.VMEM((CHIPS, 16, HD), f32),
            pltpu.VMEM((CHIPS, 16, HD), bf16),
        ),
        in_specs=[VMEM] * 7,
        out_specs=(VMEM,) * 3,
        scratch_shapes=[pltpu.VMEM((image, HD), f32), pltpu.VMEM((image, HD), f32)],
        compiler_params=pltpu.CompilerParams(vmem_limit_bytes=36 * 2**20),
        name="gradients",
    )(live_tiles, in_vmem(expo), in_vmem(d_prob), in_vmem(stats), kv_3, q, d_live)
    other = lax.ppermute(send, "c", [(0, 1), (1, 0)])
    d_queries = pl.pallas_call(
        query_kernel,
        out_shape=jax.ShapeDtypeStruct(queries.shape, bf16),
        in_specs=[VMEM] * 6,
        out_specs=VMEM,
        compiler_params=pltpu.CompilerParams(vmem_limit_bytes=16 * 2**20),
        cost_estimate=pl.CostEstimate(
            flops=2 * rows * width_q * image, bytes_accessed=4 * rows * width_q, transcendentals=0
        ),
        name="query_gradient",
    )(factor, kv_0, kv_1, kv_2, kv_3, in_vmem(d_score))
    partial = pl.pallas_call(
        chip_kernel,
        out_shape=pltpu.VMEM((CHIPS, 16, HD), bf16),
        in_specs=[VMEM, VMEM, HBM],
        out_specs=VMEM,
        name="add_cores",
    )(in_vmem(keep), in_vmem(other), in_hbm(d_queries))
    run = CHIPS // BLOCKS
    members = [(zh ^ FIRST_ZH) * run + (i ^ FIRST_IN) for zh in range(BLOCKS) for i in range(run)]
    pieces = lax.all_to_all(partial, ("zh", "x", "zl"), 0, 0, axis_index_groups=[members])
    d_keys, d_values = pl.pallas_call(
        sum_kernel,
        out_shape=(jax.ShapeDtypeStruct((8, width), f32),) * 2,
        in_specs=[VMEM, VMEM],
        out_specs=(VMEM, VMEM),
        name="add_up",
    )(factor, in_vmem(pieces))
    return d_queries, d_keys, d_values


def solution(mesh):
    mesh = Mesh(mesh.devices.reshape(SIZES), AXES)
    section, tensor = ("y", "zh"), ("x", "zl", "c")
    in_specs = (
        P(section, tensor),
        P(section, None),
        P(section, None),
        P(section, tensor),
        P(),
        P(),
        P(),
    )
    out_specs = (P(section, tensor), P(AXES, None), P(AXES, None))
    return jax.shard_map(local, mesh=mesh, in_specs=in_specs, out_specs=out_specs, check_vma=False)
```

```python
import jax
import jax.numpy as jnp
from jax import lax
from jax.experimental import pallas as pl
from jax.experimental.pallas import tpu as pltpu
from jax.sharding import Mesh, PartitionSpec as P

HD = 128
TILE = 128
SCALE = HD**-0.5
LOG2E = 1.4426950408889634
AXES = ("y", "zh", "x", "zl", "c")
SIZES = (8, 4, 4, 2, 2)
BLOCKS = 4
HEADS_X = 2
HEADS_STEP = 2
CHIPS = 32
GROUPS = ((1, 2, 4, 7), (0, 3, 5, 6))
FIRST_ZH, FIRST_IN = 2, 5
NT = (((1,), (1,)), ((), ()))
VMEM = pl.BlockSpec(memory_space=pltpu.VMEM)
HBM = pl.BlockSpec(memory_space=pltpu.HBM)


def partner(zh, c):
    return lax.bitwise_xor(zh, 3 - c)


def end_of(zh):
    return jnp.where((zh == 0) | (zh == BLOCKS - 1), 1, 0)


def pick_kernel(keys, values, own, first, second, blocks, sems):
    x, zh, zl, c = (lax.axis_index(axis) for axis in ("x", "zh", "zl", "c"))
    copies = [
        pltpu.make_async_copy(source, blocks.at[k], sems.at[k])
        for k, source in enumerate((keys, values))
    ]
    for copy in copies:
        copy.start()
    flip = lax.rem(end_of(zh) + zl, 2)
    for k in range(2):
        copies[k].wait()
        for section, out in ((zh, own), (partner(zh, c), first), (lax.bitwise_xor(zh, 1), second)):
            head = x * HEADS_X + lax.rem(end_of(section) + flip, 2)
            out[k] = blocks[k, :, pl.ds(pl.multiple_of(head * HD, HD), HD)]


def prepare_kernel(
    tiles, text_len, queries, d_out, gate, q_out, d_live, live_tiles, factor, s_tiles, s_text, q, d, sems
):
    pairs = ((d_out, d), (queries, q), (text_len, s_text), (tiles, s_tiles))
    copies = [pltpu.make_async_copy(*pair, sems.at[i]) for i, pair in enumerate(pairs)]
    for copy in copies:
        copy.start()
    for copy in copies:
        copy.wait()
    y, zh = lax.axis_index("y"), lax.axis_index("zh")
    live_tiles[...] = jnp.full(live_tiles.shape, s_tiles[y], jnp.int32)
    factor[...] = jnp.broadcast_to(jnp.tanh(gate[...]), factor.shape)
    rows, heads = queries.shape[0], queries.shape[1] // HD
    live = lax.broadcasted_iota(jnp.int32, (rows, HD), 0) + zh * rows < s_text[y]
    for h in range(heads):
        cols = pl.ds(h * HD, HD)
        step, place = h // HEADS_STEP, pl.ds(h % HEADS_STEP * rows, rows)
        q_out[step, place] = q[:, cols]
        d_live[step, place] = jnp.where(live, d[:, cols].astype(jnp.float32), 0.0).astype(jnp.bfloat16)


def stacked(parts, k):
    return jnp.concatenate([part[k] for part in parts], 0)


def products(parts, q, s):
    score = lax.dot_general(stacked(parts, 0), q, NT, preferred_element_type=jnp.float32)
    d_prob = lax.dot_general(stacked(parts, 1), s, NT, preferred_element_type=jnp.float32)
    return score, d_prob


def largest(score, live):
    top = -3e38
    for b in range(len(live)):
        part = jnp.max(score[b * TILE : (b + 1) * TILE], axis=0, keepdims=True)
        top = jnp.maximum(top, jnp.where(live[b], part, -3e38))
    return top


def exponentials(score, top, live):
    parts = []
    for b in range(len(live)):
        shift = jnp.where(live[b], top, 1e30)
        parts.append(jnp.exp2((score[b * TILE : (b + 1) * TILE] - shift) * (SCALE * LOG2E)))
    return jnp.concatenate(parts, 0)


def places():
    zh, c = lax.axis_index("zh"), lax.axis_index("c")
    return zh, partner(zh, c), lax.bitwise_xor(zh, 1), partner(zh, 1 - c)


def first_kernel(live_tiles, kv_0, kv_1, kv_2, queries, d_out, expo_out, d_prob_out, stats):
    live = [place < live_tiles[0:1, 0:1] for place in places()[:3]]
    kv = (kv_0, kv_1, kv_2)
    steps = queries.shape[0]
    ahead = products(kv, queries[0], d_out[0])
    for step in range(steps):
        score, d_prob = ahead
        if step < steps - 1:
            ahead = products(kv, queries[step + 1], d_out[step + 1])
        top = largest(score, live)
        expo = exponentials(score, top, live)
        expo_out[step] = expo
        d_prob_out[step] = d_prob
        stats[step, 0:1] = top
        stats[step, 1:2] = jnp.sum(expo, axis=0, keepdims=True)
        stats[step, 2:3] = jnp.sum(expo * d_prob, axis=0, keepdims=True)


def main_kernel(
    live_tiles, expo_1, d_prob_1, stats, kv_3, queries, d_out, d_score, keep, send, acc_k, acc_v
):
    f32, bf16 = jnp.float32, jnp.bfloat16
    live = [place < live_tiles[0:1, 0:1] for place in places()[3:]]
    kv = (kv_3,)
    steps, before = queries.shape[0], expo_1.shape[1]
    ahead = products(kv, queries[0], d_out[0])
    for step in range(steps):
        q, s = queries[step], d_out[step]
        score, d_prob = ahead
        if step < steps - 1:
            ahead = products(kv, queries[step + 1], d_out[step + 1])
        top_1, sum_1, dot_1 = (stats[step, i : i + 1] for i in range(3))
        top = jnp.maximum(top_1, largest(score, live))
        expo = exponentials(score, top, live)
        weight = jnp.exp2((top_1 - top) * (SCALE * LOG2E))
        inverse = 1.0 / (sum_1 * weight + jnp.sum(expo, axis=0, keepdims=True))
        delta = (dot_1 * weight + jnp.sum(expo * d_prob, axis=0, keepdims=True)) * inverse
        prob_1 = (expo_1[step] * (weight * inverse)).astype(bf16)
        prob_2 = (expo * inverse).astype(bf16)
        d_s_1 = prob_1 * (d_prob_1[step] - delta).astype(bf16)
        d_s_2 = prob_2 * (d_prob - delta).astype(bf16)
        d_score[step, :before] = d_s_1
        d_score[step, before:] = d_s_2
        term_k = jnp.dot(jnp.concatenate([d_s_1, d_s_2], 0), q, preferred_element_type=f32)
        term_v = jnp.dot(jnp.concatenate([prob_1, prob_2], 0), s, preferred_element_type=f32)
        if step == 0:
            acc_k[...] = term_k
            acc_v[...] = term_v
        else:
            acc_k[...] += term_k
            acc_v[...] += term_v
    both = [acc.reshape(CHIPS, 2, 8, HD) for acc in (acc_k[...], acc_v[...])]
    both = jnp.concatenate(both, 2)
    even = lax.axis_index("c") == 0
    mine, other = jnp.where(even, both[:, 0], both[:, 1]), jnp.where(even, both[:, 1], both[:, 0])
    other = other.astype(bf16)
    run = CHIPS // BLOCKS
    for b, place in enumerate(places()):
        for i in range(run):
            at = pl.ds(lax.bitwise_xor(place, FIRST_ZH) * run + (i ^ FIRST_IN), 1)
            keep[at] = mine[b * run + i : b * run + i + 1]
            send[at] = other[b * run + i : b * run + i + 1]


def chip_kernel(keep, other, _, partial):
    partial[...] = (keep[...] + other[...].astype(jnp.float32)).astype(jnp.bfloat16)


def query_kernel(gate_factor, kv_0, kv_1, kv_2, kv_3, d_score, d_queries, result, sems):
    factor = gate_factor[0:1, 0:1] * SCALE
    keys_t = stacked((kv_0, kv_1, kv_2, kv_3), 0).T
    rows = d_queries.shape[0]
    copies = []
    for step in range(d_score.shape[0]):
        d_q = jnp.dot(keys_t, d_score[step], preferred_element_type=jnp.float32)
        d_q = (d_q * factor).T.astype(jnp.bfloat16)
        for i in range(HEADS_STEP):
            cols = pl.ds((step * HEADS_STEP + i) * HD, HD)
            result[:, cols] = d_q[i * rows : (i + 1) * rows]
        cols = pl.ds(step * HEADS_STEP * HD, HEADS_STEP * HD)
        copies.append(pltpu.make_async_copy(result.at[:, cols], d_queries.at[:, cols], sems.at[step]))
        copies[-1].start()
    for copy in copies:
        copy.wait()


def sum_kernel(gate_factor, pieces, d_keys, d_values):
    factor = gate_factor[0:1]
    heads = CHIPS // BLOCKS
    for head in range(heads):
        total = None
        for zh in range(BLOCKS):
            piece = pieces[zh * heads + (head ^ FIRST_IN)].astype(jnp.float32)
            total = piece if total is None else total + piece
        cols = pl.ds(head * HD, HD)
        d_keys[:, cols] = total[:8] * (factor * SCALE)
        d_values[:, cols] = total[8:] * factor


def in_vmem(array):
    return pltpu.with_memory_space_constraint(array, pltpu.VMEM)


def in_hbm(array):
    return pltpu.with_memory_space_constraint(array, pltpu.HBM)


def swap(value, step):
    pairs = []
    for c in range(2):
        for group in GROUPS:
            pairs += [(2 * group[i] + c, 2 * group[i ^ step[c]] + c) for i in range(BLOCKS)]
    return in_vmem(lax.ppermute(value, ("zh", "zl", "c"), pairs))


def local(queries, keys, values, d_out, gate, tiles, text_len):
    f32, bf16 = jnp.float32, jnp.bfloat16
    gate = gate.reshape(1, 1)
    block, width = keys.shape
    rows, width_q = queries.shape
    steps = width_q // HD // HEADS_STEP
    image = BLOCKS * block
    own, first, second = pl.pallas_call(
        pick_kernel,
        out_shape=(pltpu.VMEM((2, block, HD), bf16),) * 3,
        in_specs=[HBM, HBM],
        out_specs=(VMEM,) * 3,
        scratch_shapes=[pltpu.VMEM((2, block, width), bf16), pltpu.SemaphoreType.DMA((2,))],
        name="pick",
    )(in_hbm(keys), in_hbm(values))
    kv_0, kv_1, kv_2 = in_vmem(own), swap(first, (3, 2)), swap(second, (1, 1))
    kv_3 = in_vmem(lax.ppermute(kv_1, "c", [(0, 1), (1, 0)]))
    by_step = (steps, rows * HEADS_STEP, HD)
    q, d_live, live_tiles, factor = pl.pallas_call(
        prepare_kernel,
        out_shape=(
            pltpu.VMEM(by_step, bf16),
            pltpu.VMEM(by_step, bf16),
            pltpu.VMEM((8, HD), jnp.int32),
            pltpu.VMEM((8, HD), f32),
        ),
        in_specs=[HBM] * 4 + [VMEM],
        out_specs=(VMEM,) * 4,
        scratch_shapes=[
            pltpu.SMEM(tiles.shape, jnp.int32),
            pltpu.SMEM(text_len.shape, jnp.int32),
            pltpu.VMEM(queries.shape, bf16),
            pltpu.VMEM(queries.shape, bf16),
            pltpu.SemaphoreType.DMA((4,)),
        ],
        compiler_params=pltpu.CompilerParams(vmem_limit_bytes=16 * 2**20),
        cost_estimate=pl.CostEstimate(
            flops=4 * rows * width_q, bytes_accessed=8 * rows * width_q, transcendentals=0
        ),
        name="prepare",
    )(*(in_hbm(array) for array in (tiles, text_len, queries, d_out)), gate)
    q, d_live, live_tiles, factor = (in_vmem(array) for array in (q, d_live, live_tiles, factor))
    by_part = (steps, image - block, rows * HEADS_STEP)
    expo, d_prob, stats = pl.pallas_call(
        first_kernel,
        out_shape=(
            pltpu.VMEM(by_part, f32),
            pltpu.VMEM(by_part, f32),
            pltpu.VMEM((steps, 8, rows * HEADS_STEP), f32),
        ),
        in_specs=[VMEM] * 6,
        out_specs=(VMEM,) * 3,
        compiler_params=pltpu.CompilerParams(vmem_limit_bytes=24 * 2**20),
        cost_estimate=pl.CostEstimate(
            flops=40 * rows * width_q * image, bytes_accessed=rows * width_q, transcendentals=0
        ),
        name="three_blocks",
    )(live_tiles, kv_0, kv_1, kv_2, q, d_live)
    d_score, keep, send = pl.pallas_call(
        main_kernel,
        out_shape=(
            pltpu.VMEM((steps, image, rows * HEADS_STEP), bf16),
            pltpu.VMEM((CHIPS, 16, HD), f32),
            pltpu.VMEM((CHIPS, 16, HD), bf16),
        ),
        in_specs=[VMEM] * 7,
        out_specs=(VMEM,) * 3,
        scratch_shapes=[pltpu.VMEM((image, HD), f32), pltpu.VMEM((image, HD), f32)],
        compiler_params=pltpu.CompilerParams(vmem_limit_bytes=36 * 2**20),
        name="gradients",
    )(live_tiles, in_vmem(expo), in_vmem(d_prob), in_vmem(stats), kv_3, q, d_live)
    other = lax.ppermute(send, "c", [(0, 1), (1, 0)])
    d_queries = pl.pallas_call(
        query_kernel,
        out_shape=jax.ShapeDtypeStruct(queries.shape, bf16),
        in_specs=[VMEM] * 6,
        out_specs=HBM,
        scratch_shapes=[pltpu.VMEM(queries.shape, bf16), pltpu.SemaphoreType.DMA((steps,))],
        compiler_params=pltpu.CompilerParams(vmem_limit_bytes=16 * 2**20),
        cost_estimate=pl.CostEstimate(
            flops=2 * rows * width_q * image, bytes_accessed=4 * rows * width_q, transcendentals=0
        ),
        name="query_gradient",
    )(factor, kv_0, kv_1, kv_2, kv_3, in_vmem(d_score))
    partial = pl.pallas_call(
        chip_kernel,
        out_shape=pltpu.VMEM((CHIPS, 16, HD), bf16),
        in_specs=[VMEM, VMEM, HBM],
        out_specs=VMEM,
        name="add_cores",
    )(in_vmem(keep), in_vmem(other), in_hbm(d_queries))
    run = CHIPS // BLOCKS
    members = [(zh ^ FIRST_ZH) * run + (i ^ FIRST_IN) for zh in range(BLOCKS) for i in range(run)]
    pieces = lax.all_to_all(partial, ("zh", "x", "zl"), 0, 0, axis_index_groups=[members])
    d_keys, d_values = pl.pallas_call(
        sum_kernel,
        out_shape=(jax.ShapeDtypeStruct((8, width), f32),) * 2,
        in_specs=[VMEM, VMEM],
        out_specs=(VMEM, VMEM),
        name="add_up",
    )(factor, in_vmem(pieces))
    return d_queries, d_keys, d_values


def solution(mesh):
    mesh = Mesh(mesh.devices.reshape(SIZES), AXES)
    section, tensor = ("y", "zh"), ("x", "zl", "c")
    in_specs = (
        P(section, tensor),
        P(section, None),
        P(section, None),
        P(section, tensor),
        P(),
        P(),
        P(),
    )
    out_specs = (P(section, tensor), P(AXES, None), P(AXES, None))
    return jax.shard_map(local, mesh=mesh, in_specs=in_specs, out_specs=out_specs, check_vma=False)
```
